32 devices in a mesh: rep: 2 (over core), src: 8 (over z, x), tgt: 2 (over y).
Axes of the slice: x: 2, y: 2, z: 4, core: 2. Of those that a mesh axis runs over, the one named last changes fastest.
Arguments:
- src_feats: float32 [2, 256, 3200], P('rep', ('src', 'tgt')), may hold values from -6 to 6
- tgt_cotangent: float32 [2, 256, 3200], P('rep', ('tgt', 'src')), may hold values from -0.6 to 0.6
- rotation: float32 [2, 8, 2, 115, 384], P('rep', 'src', 'tgt'), may hold values from -3 to 3
- edge_src: int32 [2, 8, 2, 384], P('rep', 'src', 'tgt'), may hold values from 0 to 31
- edge_tgt: int32 [2, 8, 2, 384], P('rep', 'src', 'tgt'), may hold values from 0 to 127
- edge_count: int32 [2, 8, 2], P('rep', 'src', 'tgt'), may hold values from 192 to 384, as said below
- w_zero: float32 [640, 640], replicated, may hold values from -0.25 to 0.25
- w_one_re: float32 [512, 512], replicated, may hold values from -0.1875 to 0.1875
- w_one_im: float32 [512, 512], replicated, may hold values from -0.1875 to 0.1875
- w_two_re: float32 [384, 384], replicated, may hold values from -0.21875 to 0.21875
- w_two_im: float32 [384, 384], replicated, may hold values from -0.21875 to 0.21875
Outputs:
- grad_feats: float32 [2, 256, 3200], P('rep', ('src', 'tgt'))
- grad_w_zero: float32 [640, 640], P('src')
- grad_w_one_re: float32 [512, 512], P('src')
- grad_w_one_im: float32 [512, 512], P('src')
- grad_w_two_re: float32 [384, 384], P('src')
- grad_w_two_im: float32 [384, 384], P('src')
The draws below stay inside these ranges and needn't reach their ends.
Inputs may be any that keep to these rules, and one draw needn't show every extreme that they name: `edge_count`: some tile of each structure is full.
All inputs are finite; a program needn't handle non-finite values.
Results may differ from the reference program's by a relative error of at most 0.0003.
Values sent between devices are 32-bit elements; how exact they have to be, the bound alone decides.
No kernel may reach another device: no remote copies, remote signals or barrier semaphores. Data moves between devices by JAX's collectives and lax.ppermute only.
A program may use at most 128 MiB of HBM per device.

```python
import jax
import jax.numpy as jnp
from jax import lax

CH = 128
ROT = 115
EDGE_CAP = 384
STRUCTS = 2
ATOMS = 256
SRC_BLK = 32
TGT_BLK = 128
FEAT = 3200
N_SRC = 8
N_TGT = 2


def draw_edge_src(key, part):
    return jax.random.randint(jax.random.fold_in(key, 11), (STRUCTS, N_SRC, N_TGT, EDGE_CAP), 0, SRC_BLK, dtype=jnp.int32)


def draw_edge_tgt(key, part):
    return jax.random.randint(jax.random.fold_in(key, 23), (STRUCTS, N_SRC, N_TGT, EDGE_CAP), 0, TGT_BLK, dtype=jnp.int32)


def draw_edge_count(key, part):
    first, third = jax.random.split(jax.random.fold_in(key, 37), 2)
    tiles = N_SRC * N_TGT
    base = jax.random.randint(first, (STRUCTS, tiles), EDGE_CAP // 2, EDGE_CAP + 1, dtype=jnp.int32)
    picked = jax.random.randint(third, (STRUCTS, 1), 0, tiles, dtype=jnp.int32)
    full = jnp.arange(tiles, dtype=jnp.int32)[None, :] == picked
    counts = jnp.where(full, EDGE_CAP, base).astype(jnp.int32)
    return counts.reshape(STRUCTS, N_SRC, N_TGT)


def block_scale(stream_key, dims, cuts, least, top_value):
    gain, own = 1.0, jax.random.fold_in(stream_key, 6)
    for dim, blocks in cuts:
        heights = jnp.exp(jax.random.uniform(jax.random.fold_in(own, dim), (blocks,), jnp.float32, least / len(cuts), top_value / len(cuts)))
        gain = gain * jnp.repeat(heights, dims[dim] // blocks).reshape([-1 if axis == dim else 1 for axis in range(len(dims))])
    return gain


def gaussian(stream_key, dims, spread, limit, shards=(), kind=jnp.bfloat16):
    array = jax.random.normal(stream_key, dims, jnp.float32) * spread
    if len(shards) > 0:
        array = block_scale(stream_key, dims, shards, -0.22, 0.18) * array
    return jnp.clip(array, min=-limit, max=limit).astype(kind)


def setup_inputs(seed: int = 0) -> dict:
    splits = jax.random.split(jax.random.key(seed), 12)
    return {
        "src_feats": gaussian(splits[0], (STRUCTS, ATOMS, FEAT), 1.0, 6.0, ((0, 2), (1, 16)), jnp.float32),
        "tgt_cotangent": gaussian(splits[1], (STRUCTS, ATOMS, FEAT), 0.1, 0.6, ((0, 2), (1, 16)), jnp.float32),
        "rotation": gaussian(splits[2], (STRUCTS, N_SRC, N_TGT, ROT, EDGE_CAP), 0.45, 3.0, ((0, 2), (1, 8), (2, 2)), jnp.float32),
        "edge_src": draw_edge_src(jax.random.fold_in(splits[11], 71), 0),
        "edge_tgt": draw_edge_tgt(jax.random.fold_in(splits[11], 71), 0),
        "edge_count": draw_edge_count(jax.random.fold_in(splits[11], 71), 0),
        "w_zero": gaussian(splits[6], (5 * CH, 5 * CH), (5 * CH) ** -0.5, 0.25, (), jnp.float32),
        "w_one_re": gaussian(splits[7], (4 * CH, 4 * CH), (8 * CH) ** -0.5, 0.1875, (), jnp.float32),
        "w_one_im": gaussian(splits[8], (4 * CH, 4 * CH), (8 * CH) ** -0.5, 0.1875, (), jnp.float32),
        "w_two_re": gaussian(splits[9], (3 * CH, 3 * CH), (6 * CH) ** -0.5, 0.21875, (), jnp.float32),
        "w_two_im": gaussian(splits[10], (3 * CH, 3 * CH), (6 * CH) ** -0.5, 0.21875, (), jnp.float32),
    }


OFFSETS = (0, 1, 10, 35, 70)
HIGH = lax.Precision.HIGHEST


def rotations(wig):
    mats = []
    for level in range(5):
        order = min(level, 2)
        rows = 2 * order + 1
        cols = 2 * level + 1
        piece = wig[OFFSETS[level]:OFFSETS[level] + rows * cols]
        mats.append(piece.reshape(rows, cols, piece.shape[-1]))
    return mats


def group(rotated, count):
    zero = jnp.stack([rotated[v][:, min(v, 2)] for v in range(5)], 1)
    plus_one = jnp.stack([rotated[v][:, min(v, 2) + 1] for v in range(1, 5)], 1)
    minus_one = jnp.stack([rotated[v][:, min(v, 2) - 1] for v in range(1, 5)], 1)
    plus_two = jnp.stack([rotated[v][:, 4] for v in range(2, 5)], 1)
    minus_two = jnp.stack([rotated[v][:, 0] for v in range(2, 5)], 1)
    return tuple(a.reshape(count, -1) for a in (zero, plus_one, minus_one, plus_two, minus_two))


def ungroup(groups, count, chans):
    zero, plus_one, minus_one, plus_two, minus_two = [a.reshape(count, -1, chans) for a in groups]
    result = []
    for level in range(5):
        rows = []
        if level >= 2:
            rows.append(minus_two[:, level - 2])
        if level >= 1:
            rows.append(minus_one[:, level - 1])
        rows.append(zero[:, level])
        if level >= 1:
            rows.append(plus_one[:, level - 1])
        if level >= 2:
            rows.append(plus_two[:, level - 2])
        result.append(jnp.stack(rows, 1))
    return result


def tdot(left, right):
    return lax.dot_general(left, right, (((0,), (0,)), ((), ())), precision=HIGH, preferred_element_type=jnp.float32)


def ntdot(left, right):
    return lax.dot_general(left, right, (((1,), (1,)), ((), ())), precision=HIGH, preferred_element_type=jnp.float32)


def block_grads(xrows, grows, wig, weights):
    w_zero, w_one_re, w_one_im, w_two_re, w_two_im = weights
    count, coefs, chans = xrows.shape
    mats = rotations(wig)
    xrot = [jnp.einsum('rcb,bcf->brf', mats[v], xrows[:, v * v:(v + 1) * (v + 1)], precision=HIGH) for v in range(5)]
    grot = [jnp.einsum('rcb,bcf->brf', mats[v], grows[:, v * v:(v + 1) * (v + 1)], precision=HIGH) for v in range(5)]
    z0, zp1, zm1, zp2, zm2 = group(xrot, count)
    u0, up1, um1, up2, um2 = group(grot, count)
    grads = (tdot(z0, u0), tdot(zp1, up1) + tdot(zm1, um1), tdot(zp1, um1) - tdot(zm1, up1),
             tdot(zp2, up2) + tdot(zm2, um2), tdot(zp2, um2) - tdot(zm2, up2))
    d0 = ntdot(u0, w_zero)
    dp1 = ntdot(up1, w_one_re) + ntdot(um1, w_one_im)
    dm1 = ntdot(um1, w_one_re) - ntdot(up1, w_one_im)
    dp2 = ntdot(up2, w_two_re) + ntdot(um2, w_two_im)
    dm2 = ntdot(um2, w_two_re) - ntdot(up2, w_two_im)
    back = ungroup((d0, dp1, dm1, dp2, dm2), count, chans)
    pieces = [jnp.einsum('rcb,brf->bcf', mats[v], back[v], precision=HIGH) for v in range(5)]
    return jnp.concatenate(pieces, 1), grads


def reference(src_feats, tgt_cotangent, rotation, edge_src, edge_tgt, edge_count, w_zero, w_one_re, w_one_im, w_two_re, w_two_im):
    weights = (w_zero, w_one_re, w_one_im, w_two_re, w_two_im)
    structs, atoms, feat = src_feats.shape
    chans = w_zero.shape[0] // 5
    nsrc, ntgt, cap = edge_src.shape[1], edge_src.shape[2], edge_src.shape[3]
    src_blk = atoms // nsrc
    tgt_blk = atoms // ntgt
    grads = tuple(jnp.zeros(w.shape, jnp.float32) for w in weights)
    outputs = []
    for which in range(structs):
        xall = src_feats[which].reshape(atoms, 25, chans)
        gall = tgt_cotangent[which].reshape(atoms, 25, chans)

        def tile(carry, index):
            total, sums = carry
            row = index // ntgt
            col = index % ntgt
            sources = (edge_src[which][row, col] + row * src_blk).astype(jnp.int32)
            targets = (edge_tgt[which][row, col] + col * tgt_blk).astype(jnp.int32)
            live = (jnp.arange(cap, dtype=jnp.int32) < edge_count[which][row, col]).astype(jnp.float32)
            xrows = xall[sources] * live[:, None, None]
            grows = gall[targets] * live[:, None, None]
            term, parts = block_grads(xrows, grows, rotation[which][row, col], weights)
            total = total.at[sources].add(term)
            return (total, tuple(a + b for a, b in zip(sums, parts))), None

        init = (jnp.zeros((atoms, 25, chans), jnp.float32), grads)
        (total, grads), unused = lax.scan(tile, init, jnp.arange(nsrc * ntgt, dtype=jnp.int32))
        outputs.append(total.reshape(atoms, feat))
    grad_feats = jnp.stack(outputs, 0)
    return (grad_feats, grads[0], grads[1], grads[2], grads[3], grads[4])
```

```python
import functools

import jax
import jax.numpy as jnp
from jax import lax
from jax.experimental import pallas as pl
from jax.experimental.pallas import tpu as pltpu
from jax.sharding import PartitionSpec as P

OFFSETS = (0, 1, 10, 35, 70)
ROT = 115
LANES = 128
AXES = ("rep", "src", "tgt")
F32 = jnp.float32
BF16 = jnp.bfloat16

GROUPS = (5, 4, 4, 3, 3)
STARTS = (0, 5, 9, 13, 16)


def place(level, order):
    group = {0: 0, 1: 1, -1: 2, 2: 3, -2: 4}[order]
    return STARTS[group] + level - abs(order)


def split(value):
    high = value.astype(BF16)
    return high, (value - high.astype(F32)).astype(BF16)


def nt(left, right):
    return lax.dot_general(left, right, (((1,), (1,)), ((), ())), preferred_element_type=F32)


def tn(left, right):
    return lax.dot_general(left, right, (((0,), (0,)), ((), ())), preferred_element_type=F32)


def nn(left, right):
    return lax.dot_general(left, right, (((1,), (0,)), ((), ())), preferred_element_type=F32)


def onehot(row, atoms, shard, mine, flip, twice=True):
    ids = row.astype(jnp.int32)
    bits = shard.bit_length() - 1
    rel = lax.shift_right_arithmetic(ids, bits) ^ mine
    if flip is not None:
        pair = rel & 3
        swapped = lax.shift_right_logical(pair, 1) | lax.shift_left(pair & 1, 1)
        rel = jnp.where(flip != 0, (rel & ~3) | swapped, rel)
    where = jnp.where(ids < 0, -1, lax.shift_left(rel, bits) | (ids & (shard - 1)))
    hit = lax.broadcasted_iota(jnp.int32, (atoms, row.shape[1]), 0) == where
    one = jnp.where(hit, 1.0, 0.0).astype(BF16)
    return jnp.concatenate([one, one], 0) if twice else one


def gather(shards, select, out, chans):
    for level in range(5):
        first, last = level * level * chans, (level + 1) * (level + 1) * chans
        rows = jnp.concatenate([s[:, first:last] for s in shards], 0)
        high, low = split(rows)
        out[first:last, :] = tn(jnp.concatenate([high, low], 0), select)


def spread(pack, out):
    for k in range(ROT):
        out[k] = jnp.broadcast_to(pack[k : k + 1, :], (8, pack.shape[1]))


def rotate(rot, feats, base, store, chans):
    edges = rot.shape[2]
    tiles = edges // LANES

    def body(step, carry):
        tile = step % tiles
        strip = step // tiles
        lanes = pl.ds(pl.multiple_of(tile * LANES, LANES), LANES)
        wide = pl.ds(pl.multiple_of(base + tile * LANES, LANES), LANES)
        for level in range(5):
            order = min(level, 2)
            cols = 2 * level + 1
            acc = [[None, None] for _ in range(2 * order + 1)]
            for c in range(cols):
                row = pl.multiple_of((level * level + c) * chans + strip * 16, 16)
                x = feats[pl.ds(row, 16), wide]
                for r in range(2 * order + 1):
                    factor = rot[OFFSETS[level] + r * cols + c, :, lanes]
                    for half in range(2):
                        term = factor * x[half * 8 : half * 8 + 8]
                        acc[r][half] = term if c == 0 else acc[r][half] + term
            for r in range(2 * order + 1):
                store(place(level, r - order), strip, wide, jnp.concatenate(acc[r], 0))
        return carry

    lax.fori_loop(0, (chans // 16) * tiles, body, 0)


def source_kernel(count, shard, own_slots, chans, me, *refs):
    shards = (refs[:count], refs[count : 2 * count])
    packs = refs[2 * count : 2 * count + 2]
    high_out, low_out, feats, rot, full, picked = refs[2 * count + 2 :]
    edges = packs[0].shape[1]
    mine, owner = me[1], me[0]
    rows = tuple(g * chans // (2 * own_slots) for g in GROUPS)
    for tile in range(2):
        select = onehot(packs[tile][ROT : ROT + 1, :], count * shard, shard, mine, None)
        gather(shards[tile], select, feats, chans)
        spread(packs[tile], rot)

        def store(where, strip, lanes, value):
            full[pl.ds(pl.multiple_of(where * chans + strip * 16, 16), 16), lanes] = value

        rotate(rot, feats, 0, store, chans)
        at = 0
        for group in range(5):
            for slot in range(own_slots):
                owned = owner ^ (2 * slot)
                source = pl.multiple_of(STARTS[group] * chans + owned * rows[group], 8)
                picked[at : at + rows[group], :] = full[pl.ds(source, rows[group]), :]
                at += rows[group]
        high, low = split(picked[...])
        high_out[:, tile * edges : (tile + 1) * edges] = high
        low_out[:, tile * edges : (tile + 1) * edges] = low


def weight_kernel(count, shard, own_slots, parts, chans, me, *refs):
    shards = refs[:count]
    packs = refs[count : count + 2]
    zh_any, zl_any = refs[count + 2 : count + 4]
    keep_any, send_any, uh_any, ul_any = refs[count + 4 : count + 8]
    feats, rot, zh, zl, uh, ul, full, load_sem, u_sem, out_sem = refs[count + 8 :]
    edges = packs[0].shape[1]
    owner, core, tgt = me[0], me[2], me[1]
    loads = [
        pltpu.make_async_copy(zh_any, zh, load_sem.at[0]),
        pltpu.make_async_copy(zl_any, zl, load_sem.at[1]),
    ]
    for load in loads:
        load.start()
    select = jnp.concatenate(
        [onehot(p[ROT + 1 : ROT + 2, :], count * shard, shard, owner, core) for p in packs], 1
    )
    gather(shards, select, feats, chans)

    def store(where, strip, lanes, value):
        high, low = split(value)
        rows = pl.ds(pl.multiple_of(where * chans + strip * 16, 16), 16)
        uh[rows, lanes] = high
        ul[rows, lanes] = low

    for tile in range(2):
        spread(packs[tile], rot)
        rotate(rot, feats, tile * edges, store, chans)
        if tile == 0:
            saves = [
                pltpu.make_async_copy(uh.at[:, 0:edges], uh_any, u_sem.at[0]),
                pltpu.make_async_copy(ul.at[:, 0:edges], ul_any, u_sem.at[1]),
            ]
            for save in saves:
                save.start()
    for load in loads:
        load.wait()

    def product(left, right):
        lo = sum(GROUPS[:left]) * chans // 2, sum(GROUPS[: left + 1]) * chans // 2
        ro = STARTS[right] * chans, (STARTS[right] + GROUPS[right]) * chans
        a, b = zh[lo[0] : lo[1], :], uh[ro[0] : ro[1], :]
        c, d = zl[lo[0] : lo[1], :], ul[ro[0] : ro[1], :]
        return nt(a, b) + nt(a, d) + nt(c, b)

    def put(at, value):
        wide = value.shape[1] // LANES
        high = value.shape[0] // own_slots // 8
        for col in range(wide):
            block = value[:, col * LANES : (col + 1) * LANES]
            full[:, at + col * high : at + (col + 1) * high] = block.reshape(own_slots, high, 8, LANES)
        return at + wide * high

    at = put(0, product(0, 0))
    at = put(at, product(1, 1) + product(2, 2))
    at = put(at, product(1, 2) - product(2, 1))
    at = put(at, product(3, 3) + product(4, 4))
    at = put(at, product(3, 4) - product(4, 3))
    total = full.shape[1]
    if at < total:
        full[:, at:total] = jnp.zeros((own_slots, total - at, 8, LANES), F32)
    piece = total // (2 * parts)
    rest = parts * own_slots // 4
    copies = []
    for side, target in ((0, keep_any), (1, send_any)):
        for part in range(parts):
            for slot in range(own_slots):
                first, second = part & 1, slot & 1
                lower = (part >> 1) * (own_slots // 2) + (slot >> 1)
                pos = jnp.where(core == side, first * 2 + second, second * 2 + first) * rest + lower
                begin = ((core ^ side) * parts + (tgt ^ part)) * piece
                copy = pltpu.make_async_copy(
                    full.at[slot, pl.ds(begin, piece)], target.at[pos], out_sem.at[len(copies)]
                )
                copy.start()
                copies.append(copy)
    for copy in copies + saves:
        copy.wait()


def dual(wh, wl, uh, ul):
    return nn(wh, uh) + nn(wh, ul) + nn(wl, uh)


def back_zero_kernel(chans, w, uh, ul, out):
    wh, wl = split(w[...])
    out[...] = dual(wh, wl, uh[0 : 5 * chans, :], ul[0 : 5 * chans, :])


def back_pair_kernel(first, groups, chans, re, im, uh, ul, out):
    size = groups * chans
    rh, rl = split(re[...])
    ih, il = split(im[...])
    p = slice(first * chans, first * chans + size)
    m = slice(first * chans + size, first * chans + 2 * size)
    out[0:size, :] = dual(rh, rl, uh[p, :], ul[p, :]) + dual(ih, il, uh[m, :], ul[m, :])
    out[size : 2 * size, :] = dual(rh, rl, uh[m, :], ul[m, :]) - dual(ih, il, uh[p, :], ul[p, :])


def scatter_kernel(count, shard, chans, me, pack, d0, d1, d2, out, rot, back):
    select = onehot(pack[ROT : ROT + 1, :], count * shard, shard, me[1], None, False)
    spread(pack, rot)
    edges = pack.shape[1]
    tiles = edges // LANES
    pieces = (d0, d1, d2)
    firsts = (0, 5, 13)

    def load(where, strip, lanes):
        which = 0 if where < 5 else 1 if where < 13 else 2
        row = pl.multiple_of((where - firsts[which]) * chans + strip * 16, 16)
        return pieces[which][pl.ds(row, 16), lanes]

    def body(step, carry):
        tile = step % tiles
        strip = step // tiles
        lanes = pl.ds(pl.multiple_of(tile * LANES, LANES), LANES)
        for level in range(5):
            order = min(level, 2)
            cols = 2 * level + 1
            d = [load(place(level, r - order), strip, lanes) for r in range(2 * order + 1)]
            for c in range(cols):
                acc = [None, None]
                for r in range(2 * order + 1):
                    factor = rot[OFFSETS[level] + r * cols + c, :, lanes]
                    for half in range(2):
                        term = factor * d[r][half * 8 : half * 8 + 8]
                        acc[half] = term if r == 0 else acc[half] + term
                row = pl.multiple_of((level * level + c) * chans + strip * 16, 16)
                back[pl.ds(row, 16), lanes] = jnp.concatenate(acc, 0)
        return carry

    lax.fori_loop(0, (chans // 16) * tiles, body, 0)
    for level in range(5):
        first, last = level * level * chans, (level + 1) * (level + 1) * chans
        high, low = split(back[first:last, :])
        total = nt(select, high) + nt(select, low)
        for part in range(count):
            out[part, :, first:last] = total[part * shard : (part + 1) * shard]


def unpack_kernel(parts, chans, me, *refs):
    mine = refs[:parts]
    other = refs[parts : 2 * parts]
    outs = refs[2 * parts : 2 * parts + 5]
    tiles = refs[2 * parts + 5]
    piece = mine[0].shape[0]
    tgt, core = me[1], me[2]
    for side, group in ((0, mine), (1, other)):
        for part in range(parts):
            begin = ((core ^ side) * parts + (tgt ^ part)) * piece
            tiles[pl.ds(begin, piece)] = group[part][...]
    at = 0
    for out in outs:
        high, wide = out.shape[0] // 8, out.shape[1] // LANES
        for col in range(wide):
            block = tiles[at : at + high].reshape(high * 8, LANES)
            out[:, col * LANES : (col + 1) * LANES] = block
            at += high


def vmem(count):
    return [pl.BlockSpec(memory_space=pltpu.VMEM)] * count


def anywhere(count):
    return [pl.BlockSpec(memory_space=pl.ANY)] * count


SMEM = [pl.BlockSpec(memory_space=pltpu.SMEM)]


def call(kernel, name, ins, outs, shapes, scratch, flops, moved):
    return pl.pallas_call(
        kernel,
        name=name,
        in_specs=ins,
        out_specs=outs,
        out_shape=shapes,
        scratch_shapes=scratch,
        compiler_params=pltpu.CompilerParams(vmem_limit_bytes=56 * 1024 * 1024),
        cost_estimate=pl.CostEstimate(flops=flops, bytes_accessed=moved, transcendentals=0),
    )


def shape(*dims, dtype=F32):
    return jax.ShapeDtypeStruct(dims, dtype)


def local(
    sizes,
    src_feats,
    tgt_cotangent,
    rotation,
    edge_src,
    edge_tgt,
    edge_count,
    w_zero,
    w_one_re,
    w_one_im,
    w_two_re,
    w_two_im,
):
    reps, nsrc, ntgt = sizes
    chans = w_zero.shape[0] // 5
    shard, feat = src_feats.shape[1], src_feats.shape[2]
    edges = edge_src.shape[-1]
    slots = nsrc // 2
    src_bits = nsrc.bit_length() - 1
    tgt_bits = ntgt.bit_length() - 1
    me_src, me_tgt, me_rep = (lax.axis_index(a).astype(jnp.int32) for a in ("src", "tgt", "rep"))
    me = jnp.stack([me_src, me_tgt, me_rep])

    def hop(value, axes, *routes):
        pairs = []
        for rep in range(reps):
            s_mask, t_mask = routes[rep % len(routes)]
            for s in range(nsrc):
                for t in range(ntgt):
                    base = rep * nsrc * ntgt
                    pairs.append((base + s * ntgt + t, base + (s ^ s_mask) * ntgt + (t ^ t_mask)))
        return lax.ppermute(value, AXES, pairs)

    def cross(value):
        half = nsrc * ntgt
        return lax.ppermute(value, AXES, [(i, (i + half) % (2 * half)) for i in range(2 * half)])

    live = jnp.arange(edges, dtype=jnp.int32) < edge_count[0, 0, 0]
    ends = jnp.stack([jnp.where(live, e[0, 0, 0], -1) for e in (edge_src, edge_tgt)]).astype(F32)
    pack = jnp.concatenate([rotation[0, 0, 0], ends, jnp.zeros((3, edges), F32)], 0)
    x_own = src_feats[0]
    g_own = tgt_cotangent[0]

    g_parts = {0: g_own}
    for bit in range(src_bits - 1, 1, -1):
        for k, part in list(g_parts.items()):
            g_parts[k | (1 << bit)] = hop(part, None, (1 << bit, 0))
    pack_other = hop(pack, None, (1, 0))
    x_other = hop(x_own, None, (1, 0))
    for k, part in list(g_parts.items()):
        g_parts[k | 1] = hop(part, None, (1, 0), (2, 0))
    x_parts = [x_own] + [hop(x_own, None, (0, t)) for t in range(1, ntgt)]
    y_parts = [x_other] + [hop(x_other, None, (0, t)) for t in range(1, ntgt)]
    for k, part in list(g_parts.items()):
        g_parts[k | 2] = hop(part, None, (2, 0), (1, 0))
    g_list = [g_parts[k] for k in range(nsrc)]

    groups = sum(GROUPS) * chans
    z_rows = groups // 2
    zh, zl = call(
        functools.partial(source_kernel, ntgt, shard, slots, chans),
        "source_rows",
        SMEM + vmem(2 * ntgt + 2),
        vmem(2),
        [shape(z_rows, 2 * edges, dtype=BF16)] * 2,
        [
            pltpu.VMEM((feat, edges), F32),
            pltpu.VMEM((ROT, 8, edges), F32),
            pltpu.VMEM((groups, edges), F32),
            pltpu.VMEM((z_rows, edges), F32),
        ],
        3_000_000_000,
        8_000_000,
    )(me, *x_parts, *y_parts, pack, pack_other)

    per_slot = sum(
        (w.shape[0] // nsrc // 8) * (w.shape[1] // LANES)
        for w in (w_zero, w_one_re, w_one_im, w_two_re, w_two_im)
    )
    piece = -(-per_slot // (reps * ntgt))
    subs = ntgt * slots
    keep, send, uh, ul = call(
        functools.partial(weight_kernel, nsrc, shard, slots, ntgt, chans),
        "weight_terms",
        SMEM + vmem(nsrc + 2) + anywhere(2),
        anywhere(4),
        [shape(subs, piece, 8, LANES)] * 2 + [shape(groups, edges, dtype=BF16)] * 2,
        [
            pltpu.VMEM((feat, 2 * edges), F32),
            pltpu.VMEM((ROT, 8, edges), F32),
            pltpu.VMEM((z_rows, 2 * edges), BF16),
            pltpu.VMEM((z_rows, 2 * edges), BF16),
            pltpu.VMEM((groups, 2 * edges), BF16),
            pltpu.VMEM((groups, 2 * edges), BF16),
            pltpu.VMEM((slots, piece * reps * ntgt, 8, LANES), F32),
            pltpu.SemaphoreType.DMA((2,)),
            pltpu.SemaphoreType.DMA((2,)),
            pltpu.SemaphoreType.DMA((2 * subs,)),
        ],
        8_000_000_000,
        12_000_000,
    )(me, *g_list, pack, pack_other, zh, zl)

    routes = [((0, 1), (2, 0)), ((2, 0), (0, 1))]
    routes += [((0, 1 << b),) * 2 for b in range(tgt_bits - 1, 0, -1)]
    routes += [((1 << b, 0),) * 2 for b in range(src_bits - 1, 1, -1)]
    held, came = keep, cross(send)
    for route in routes:
        half = held.shape[0] // 2
        sent = held[half:] + came[half:]
        held = held[:half] + came[:half]
        came = hop(sent, None, *route)
    final = held[0] + came[0]

    d0 = call(
        functools.partial(back_zero_kernel, chans),
        "back_zero", vmem(3), vmem(1)[0], shape(5 * chans, edges), [], 1_900_000_000, 4_000_000,
    )(w_zero, uh, ul)
    d1 = call(
        functools.partial(back_pair_kernel, 5, 4, chans),
        "back_one", vmem(4), vmem(1)[0], shape(8 * chans, edges), [], 3_000_000_000, 5_000_000,
    )(w_one_re, w_one_im, uh, ul)
    d2 = call(
        functools.partial(back_pair_kernel, 13, 3, chans),
        "back_two", vmem(4), vmem(1)[0], shape(6 * chans, edges), [], 1_800_000_000, 4_000_000,
    )(w_two_re, w_two_im, uh, ul)
    atoms = call(
        functools.partial(scatter_kernel, ntgt, shard, chans),
        "source_sums",
        SMEM + vmem(4),
        vmem(1)[0],
        shape(ntgt, shard, feat),
        [pltpu.VMEM((ROT, 8, edges), F32), pltpu.VMEM((feat, edges), F32)],
        3_000_000_000,
        4_000_000,
    )(me, pack, d0, d1, d2)
    for b in range(tgt_bits - 1, -1, -1):
        half = atoms.shape[0] // 2
        atoms = atoms[:half] + hop(atoms[half:], None, (0, 1 << b))
    grad_feats = atoms

    mine = [final] + [hop(final, None, (0, t)) for t in range(1, ntgt)]
    other = [cross(m) for m in mine]
    outs = call(
        functools.partial(unpack_kernel, ntgt, chans),
        "unpack",
        SMEM + vmem(2 * ntgt),
        vmem(5),
        [
            shape(w.shape[0] // nsrc, w.shape[1])
            for w in (w_zero, w_one_re, w_one_im, w_two_re, w_two_im)
        ],
        [pltpu.VMEM((piece * reps * ntgt, 8, LANES), F32)],
        1_000_000,
        1_500_000,
    )(me, *mine, *other)
    return (grad_feats, *outs)


def solution(mesh):
    placed = (
        P("rep", ("src", "tgt"), None),
        P("rep", ("tgt", "src"), None),
        P("rep", "src", "tgt", None, None),
        P("rep", "src", "tgt", None),
        P("rep", "src", "tgt", None),
        P("rep", "src", "tgt"),
        P(),
        P(),
        P(),
        P(),
        P(),
    )
    sizes = tuple(mesh.shape[a] for a in AXES)
    return jax.shard_map(
        functools.partial(local, sizes),
        mesh=mesh,
        in_specs=placed,
        out_specs=(
            P("rep", ("src", "tgt"), None),
            P("src", None),
            P("src", None),
            P("src", None),
            P("src", None),
            P("src", None),
        ),
        check_vma=False,
    )
```

```python
import functools

import jax
import jax.numpy as jnp
from jax import lax
from jax.experimental import pallas as pl
from jax.experimental.pallas import tpu as pltpu
from jax.sharding import PartitionSpec as P

OFFSETS = (0, 1, 10, 35, 70)
ROT = 115
LANES = 128
AXES = ("rep", "src", "tgt")
F32 = jnp.float32
BF16 = jnp.bfloat16

GROUPS = (5, 4, 4, 3, 3)
STARTS = (0, 5, 9, 13, 16)


def place(level, order):
    group = {0: 0, 1: 1, -1: 2, 2: 3, -2: 4}[order]
    return STARTS[group] + level - abs(order)


def split(value):
    high = value.astype(BF16)
    return high, (value - high.astype(F32)).astype(BF16)


def nt(left, right):
    return lax.dot_general(left, right, (((1,), (1,)), ((), ())), preferred_element_type=F32)


def tn(left, right):
    return lax.dot_general(left, right, (((0,), (0,)), ((), ())), preferred_element_type=F32)


def nn(left, right):
    return lax.dot_general(left, right, (((1,), (0,)), ((), ())), preferred_element_type=F32)


def onehot(row, atoms, shard, mine, flip, twice=True):
    ids = row.astype(jnp.int32)
    bits = shard.bit_length() - 1
    rel = lax.shift_right_arithmetic(ids, bits) ^ mine
    if flip is not None:
        pair = rel & 3
        swapped = lax.shift_right_logical(pair, 1) | lax.shift_left(pair & 1, 1)
        rel = jnp.where(flip != 0, (rel & ~3) | swapped, rel)
    where = jnp.where(ids < 0, -1, lax.shift_left(rel, bits) | (ids & (shard - 1)))
    hit = lax.broadcasted_iota(jnp.int32, (atoms, row.shape[1]), 0) == where
    one = jnp.where(hit, 1.0, 0.0).astype(BF16)
    return jnp.concatenate([one, one], 0) if twice else one


def gather(shards, select, out, chans):
    for level in range(5):
        first, last = level * level * chans, (level + 1) * (level + 1) * chans
        rows = jnp.concatenate([s[:, first:last] for s in shards], 0)
        high, low = split(rows)
        out[first:last, :] = tn(jnp.concatenate([high, low], 0), select)


def spread(pack, out):
    for k in range(ROT):
        out[k] = jnp.broadcast_to(pack[k : k + 1, :], (8, pack.shape[1]))


def rotate(rot, feats, base, store, chans):
    edges = rot.shape[2]
    tiles = edges // LANES

    def body(step, carry):
        tile = step % tiles
        strip = step // tiles
        lanes = pl.ds(pl.multiple_of(tile * LANES, LANES), LANES)
        wide = pl.ds(pl.multiple_of(base + tile * LANES, LANES), LANES)
        for level in range(5):
            order = min(level, 2)
            cols = 2 * level + 1
            acc = [[None, None] for _ in range(2 * order + 1)]
            for c in range(cols):
                row = pl.multiple_of((level * level + c) * chans + strip * 16, 16)
                x = feats[pl.ds(row, 16), wide]
                for r in range(2 * order + 1):
                    factor = rot[OFFSETS[level] + r * cols + c, :, lanes]
                    for half in range(2):
                        term = factor * x[half * 8 : half * 8 + 8]
                        acc[r][half] = term if c == 0 else acc[r][half] + term
            for r in range(2 * order + 1):
                store(place(level, r - order), strip, wide, jnp.concatenate(acc[r], 0))
        return carry

    lax.fori_loop(0, (chans // 16) * tiles, body, 0)


def source_kernel(count, shard, own_slots, chans, me, *refs):
    shards = refs[:count]
    pack = refs[count]
    high_out, low_out, feats, rot, full, picked = refs[count + 1 :]
    rows = tuple(g * chans // (2 * own_slots) for g in GROUPS)
    select = onehot(pack[ROT : ROT + 1, :], count * shard, shard, me[1], None)
    gather(shards, select, feats, chans)
    spread(pack, rot)

    def store(where, strip, lanes, value):
        full[pl.ds(pl.multiple_of(where * chans + strip * 16, 16), 16), lanes] = value

    rotate(rot, feats, 0, store, chans)
    at = 0
    for group in range(5):
        for slot in range(own_slots):
            owned = me[0] ^ (2 * slot)
            source = pl.multiple_of(STARTS[group] * chans + owned * rows[group], 8)
            picked[at : at + rows[group], :] = full[pl.ds(source, rows[group]), :]
            at += rows[group]
    high_out[...], low_out[...] = split(picked[...])


def weight_kernel(count, shard, own_slots, parts, chans, me, *refs):
    shards = refs[:count]
    packs = refs[count : count + 2]
    z_any = refs[count + 2 : count + 6]
    keep_any, send_any = refs[count + 6 : count + 8]
    u_any = refs[count + 8 : count + 14]
    feats, rot, zh, zl, uh, ul, full, load_sem, u_sem, out_sem = refs[count + 14 :]
    edges = packs[0].shape[1]
    owner, core, tgt = me[0], me[2], me[1]
    loads = [
        pltpu.make_async_copy(z, half.at[:, tile * edges : (tile + 1) * edges], load_sem.at[k])
        for k, (z, half, tile) in enumerate(zip(z_any, (zh, zl, zh, zl), (0, 0, 1, 1)))
    ]
    for load in loads:
        load.start()
    select = jnp.concatenate(
        [onehot(p[ROT + 1 : ROT + 2, :], count * shard, shard, owner, core) for p in packs], 1
    )
    gather(shards, select, feats, chans)

    def store(where, strip, lanes, value):
        high, low = split(value)
        rows = pl.ds(pl.multiple_of(where * chans + strip * 16, 16), 16)
        uh[rows, lanes] = high
        ul[rows, lanes] = low

    for tile in range(2):
        spread(packs[tile], rot)
        rotate(rot, feats, tile * edges, store, chans)
        if tile == 0:
            saves = []
            for k, first, last in ((0, 0, 5), (1, 5, 13), (2, 13, 19)):
                for j, half in ((0, uh), (1, ul)):
                    piece = half.at[first * chans : last * chans, 0:edges]
                    at = 2 * k + j
                    saves.append(pltpu.make_async_copy(piece, u_any[at], u_sem.at[at]))
            for save in saves:
                save.start()
    for load in loads:
        load.wait()

    def product(*terms):
        left, right = [], []
        for a, b in ((zh, uh), (zh, ul), (zl, uh)):
            for sign, z, u in terms:
                first = sum(GROUPS[:z]) * chans // 2
                value = a[first : first + GROUPS[z] * chans // 2, :]
                left.append(value if sign > 0 else -value)
                right.append(b[STARTS[u] * chans : (STARTS[u] + GROUPS[u]) * chans, :])
        return nt(jnp.concatenate(left, 1), jnp.concatenate(right, 1))

    def put(at, value):
        wide = value.shape[1] // LANES
        high = value.shape[0] // own_slots // 8
        for col in range(wide):
            block = value[:, col * LANES : (col + 1) * LANES]
            full[:, at + col * high : at + (col + 1) * high] = block.reshape(own_slots, high, 8, LANES)
        return at + wide * high

    at = put(0, product((1, 0, 0)))
    at = put(at, product((1, 1, 1), (1, 2, 2)))
    at = put(at, product((1, 1, 2), (-1, 2, 1)))
    at = put(at, product((1, 3, 3), (1, 4, 4)))
    at = put(at, product((1, 3, 4), (-1, 4, 3)))
    total = full.shape[1]
    if at < total:
        full[:, at:total] = jnp.zeros((own_slots, total - at, 8, LANES), F32)
    piece = total // (2 * parts)
    rest = parts * own_slots // 4
    copies = []
    for side, target in ((0, keep_any), (1, send_any)):
        for part in range(parts):
            for slot in range(own_slots):
                first, second = part & 1, slot & 1
                lower = (part >> 1) * (own_slots // 2) + (slot >> 1)
                pos = jnp.where(core == side, first * 2 + second, second * 2 + first) * rest + lower
                begin = ((core ^ side) * parts + (tgt ^ part)) * piece
                copy = pltpu.make_async_copy(
                    full.at[slot, pl.ds(begin, piece)], target.at[pos], out_sem.at[len(copies)]
                )
                copy.start()
                copies.append(copy)
    for copy in copies + saves:
        copy.wait()


def back_zero_kernel(w, uh, ul, out):
    wh, wl = split(w[...])
    high, low = uh[...], ul[...]
    out[...] = nn(jnp.concatenate([wh, wh, wl], 1), jnp.concatenate([high, low, high], 0))


def back_pair_kernel(re, im, uh, ul, out):
    size = re.shape[0]
    rh, rl = split(re[...])
    ih, il = split(im[...])
    ph, mh = uh[0:size, :], uh[size : 2 * size, :]
    pl_, ml = ul[0:size, :], ul[size : 2 * size, :]
    w = jnp.concatenate([rh, ih, rh, ih, rl, il], 1)
    out[0:size, :] = nn(w, jnp.concatenate([ph, mh, pl_, ml, ph, mh], 0))
    out[size : 2 * size, :] = nn(w, jnp.concatenate([mh, -ph, ml, -pl_, mh, -ph], 0))


def scatter_kernel(count, shard, chans, me, pack, d0, d1, d2, out, rot, back):
    select = onehot(pack[ROT : ROT + 1, :], count * shard, shard, me[1], None, False)
    select = jnp.concatenate([select, select], 1)
    spread(pack, rot)
    edges = pack.shape[1]
    tiles = edges // LANES
    pieces = (d0, d1, d2)
    firsts = (0, 5, 13)

    def load(where, strip, lanes):
        which = 0 if where < 5 else 1 if where < 13 else 2
        row = pl.multiple_of((where - firsts[which]) * chans + strip * 16, 16)
        return pieces[which][pl.ds(row, 16), lanes]

    def body(step, carry):
        tile = step % tiles
        strip = step // tiles
        lanes = pl.ds(pl.multiple_of(tile * LANES, LANES), LANES)
        for level in range(5):
            order = min(level, 2)
            cols = 2 * level + 1
            d = [load(place(level, r - order), strip, lanes) for r in range(2 * order + 1)]
            for c in range(cols):
                acc = [None, None]
                for r in range(2 * order + 1):
                    factor = rot[OFFSETS[level] + r * cols + c, :, lanes]
                    for half in range(2):
                        term = factor * d[r][half * 8 : half * 8 + 8]
                        acc[half] = term if r == 0 else acc[half] + term
                row = pl.multiple_of((level * level + c) * chans + strip * 16, 16)
                back[pl.ds(row, 16), lanes] = jnp.concatenate(acc, 0)
        return carry

    lax.fori_loop(0, (chans // 16) * tiles, body, 0)
    for level in range(5):
        first, last = level * level * chans, (level + 1) * (level + 1) * chans
        high, low = split(back[first:last, :])
        total = nt(select, jnp.concatenate([high, low], 1))
        for part in range(count):
            out[part, :, first:last] = total[part * shard : (part + 1) * shard]


def unpack_kernel(parts, chans, me, *refs):
    mine = refs[:parts]
    other = refs[parts : 2 * parts]
    outs = refs[2 * parts : 2 * parts + 5]
    tiles = refs[2 * parts + 5]
    piece = mine[0].shape[0]
    tgt, core = me[1], me[2]
    for side, group in ((0, mine), (1, other)):
        for part in range(parts):
            begin = ((core ^ side) * parts + (tgt ^ part)) * piece
            tiles[pl.ds(begin, piece)] = group[part][...]
    at = 0
    for out in outs:
        high, wide = out.shape[0] // 8, out.shape[1] // LANES
        for col in range(wide):
            block = tiles[at : at + high].reshape(high * 8, LANES)
            out[:, col * LANES : (col + 1) * LANES] = block
            at += high


def vmem(count):
    return [pl.BlockSpec(memory_space=pltpu.VMEM)] * count


def anywhere(count):
    return [pl.BlockSpec(memory_space=pl.ANY)] * count


SMEM = [pl.BlockSpec(memory_space=pltpu.SMEM)]


def call(kernel, name, ins, outs, shapes, scratch, micros, limit):
    return pl.pallas_call(
        kernel,
        name=name,
        in_specs=ins,
        out_specs=outs,
        out_shape=shapes,
        scratch_shapes=scratch,
        compiler_params=pltpu.CompilerParams(vmem_limit_bytes=limit * 1024 * 1024),
        cost_estimate=pl.CostEstimate(
            flops=int(micros * 1_150_000_000), bytes_accessed=100_000, transcendentals=0
        ),
    )


def shape(*dims, dtype=F32):
    return jax.ShapeDtypeStruct(dims, dtype)


def local(
    sizes,
    src_feats,
    tgt_cotangent,
    rotation,
    edge_src,
    edge_tgt,
    edge_count,
    w_zero,
    w_one_re,
    w_one_im,
    w_two_re,
    w_two_im,
):
    reps, nsrc, ntgt = sizes
    chans = w_zero.shape[0] // 5
    shard, feat = src_feats.shape[1], src_feats.shape[2]
    edges = edge_src.shape[-1]
    slots = nsrc // 2
    src_bits = nsrc.bit_length() - 1
    tgt_bits = ntgt.bit_length() - 1
    me_src, me_tgt, me_rep = (lax.axis_index(a).astype(jnp.int32) for a in ("src", "tgt", "rep"))
    me = jnp.stack([me_src, me_tgt, me_rep])

    def hop(value, axes, *routes):
        pairs = []
        for rep in range(reps):
            s_mask, t_mask = routes[rep % len(routes)]
            for s in range(nsrc):
                for t in range(ntgt):
                    base = rep * nsrc * ntgt
                    pairs.append((base + s * ntgt + t, base + (s ^ s_mask) * ntgt + (t ^ t_mask)))
        return lax.ppermute(value, AXES, pairs)

    def cross(value):
        half = nsrc * ntgt
        return lax.ppermute(value, AXES, [(i, (i + half) % (2 * half)) for i in range(2 * half)])

    live = jnp.arange(edges, dtype=jnp.int32) < edge_count[0, 0, 0]
    ends = jnp.stack([jnp.where(live, e[0, 0, 0], -1) for e in (edge_src, edge_tgt)]).astype(F32)
    pack = jnp.concatenate([rotation[0, 0, 0], ends, jnp.zeros((3, edges), F32)], 0)
    x_own = src_feats[0]
    g_own = tgt_cotangent[0]

    g_parts = {0: g_own}
    for bit in range(src_bits - 1, 1, -1):
        for k, part in list(g_parts.items()):
            g_parts[k | (1 << bit)] = hop(part, None, (1 << bit, 0))
    pack_other = hop(pack, None, (1, 0))
    x_other = hop(x_own, None, (1, 0))
    for k, part in list(g_parts.items()):
        g_parts[k | 1] = hop(part, None, (1, 0), (2, 0))
    x_parts = [x_own] + [hop(x_own, None, (0, t)) for t in range(1, ntgt)]
    y_parts = [x_other] + [hop(x_other, None, (0, t)) for t in range(1, ntgt)]
    for k, part in list(g_parts.items()):
        g_parts[k | 2] = hop(part, None, (2, 0), (1, 0))
    g_list = [g_parts[k] for k in range(nsrc)]

    groups = sum(GROUPS) * chans
    z_rows = groups // 2
    z_tiles = [
        call(
            functools.partial(source_kernel, ntgt, shard, slots, chans),
            "source_rows",
            SMEM + vmem(ntgt + 1),
            vmem(2),
            [shape(z_rows, edges, dtype=BF16)] * 2,
            [
                pltpu.VMEM((feat, edges), F32),
                pltpu.VMEM((ROT, 8, edges), F32),
                pltpu.VMEM((groups, edges), F32),
                pltpu.VMEM((z_rows, edges), F32),
            ],
            5,
            24,
        )(me, *parts, rows)
        for parts, rows in ((x_parts, pack), (y_parts, pack_other))
    ]

    per_slot = sum(
        (w.shape[0] // nsrc // 8) * (w.shape[1] // LANES)
        for w in (w_zero, w_one_re, w_one_im, w_two_re, w_two_im)
    )
    piece = -(-per_slot // (reps * ntgt))
    subs = ntgt * slots
    keep, send, *u = call(
        functools.partial(weight_kernel, nsrc, shard, slots, ntgt, chans),
        "weight_terms",
        SMEM + vmem(nsrc + 2) + anywhere(4),
        anywhere(8),
        [shape(subs, piece, 8, LANES)] * 2
        + [shape(k * chans, edges, dtype=BF16) for k in (5, 5, 8, 8, 6, 6)],
        [
            pltpu.VMEM((feat, 2 * edges), F32),
            pltpu.VMEM((ROT, 8, edges), F32),
            pltpu.VMEM((z_rows, 2 * edges), BF16),
            pltpu.VMEM((z_rows, 2 * edges), BF16),
            pltpu.VMEM((groups, 2 * edges), BF16),
            pltpu.VMEM((groups, 2 * edges), BF16),
            pltpu.VMEM((slots, piece * reps * ntgt, 8, LANES), F32),
            pltpu.SemaphoreType.DMA((4,)),
            pltpu.SemaphoreType.DMA((6,)),
            pltpu.SemaphoreType.DMA((2 * subs,)),
        ],
        14,
        44,
    )(me, *g_list, pack, pack_other, *z_tiles[0], *z_tiles[1])

    routes = [((0, 1), (2, 0)), ((2, 0), (0, 1))]
    routes += [((0, 1 << b),) * 2 for b in range(tgt_bits - 1, 0, -1)]
    routes += [((1 << b, 0),) * 2 for b in range(src_bits - 1, 1, -1)]
    held, came = keep, cross(send)
    for route in routes:
        half = held.shape[0] // 2
        sent = held[half:] + came[half:]
        held = held[:half] + came[:half]
        came = hop(sent, None, *route)
    final = held[0] + came[0]

    d0 = call(
        back_zero_kernel, "back_zero", vmem(3), vmem(1)[0], shape(5 * chans, edges), [], 3, 20
    )(w_zero, *u[0:2])
    d1 = call(
        back_pair_kernel, "back_one", vmem(4), vmem(1)[0], shape(8 * chans, edges), [], 4, 24
    )(w_one_re, w_one_im, *u[2:4])
    d2 = call(
        back_pair_kernel, "back_two", vmem(4), vmem(1)[0], shape(6 * chans, edges), [], 3, 20
    )(w_two_re, w_two_im, *u[4:6])
    atoms = call(
        functools.partial(scatter_kernel, ntgt, shard, chans),
        "source_sums",
        SMEM + vmem(4),
        vmem(1)[0],
        shape(ntgt, shard, feat),
        [pltpu.VMEM((ROT, 8, edges), F32), pltpu.VMEM((feat, edges), F32)],
        5,
        24,
    )(me, pack, d0, d1, d2)
    for b in range(tgt_bits - 1, -1, -1):
        half = atoms.shape[0] // 2
        atoms = atoms[:half] + hop(atoms[half:], None, (0, 1 << b))
    grad_feats = atoms

    mine = [final] + [hop(final, None, (0, t)) for t in range(1, ntgt)]
    other = [cross(m) for m in mine]
    outs = call(
        functools.partial(unpack_kernel, ntgt, chans),
        "unpack",
        SMEM + vmem(2 * ntgt),
        vmem(5),
        [
            shape(w.shape[0] // nsrc, w.shape[1])
            for w in (w_zero, w_one_re, w_one_im, w_two_re, w_two_im)
        ],
        [pltpu.VMEM((piece * reps * ntgt, 8, LANES), F32)],
        2,
        8,
    )(me, *mine, *other)
    return (grad_feats, *outs)


def solution(mesh):
    placed = (
        P("rep", ("src", "tgt"), None),
        P("rep", ("tgt", "src"), None),
        P("rep", "src", "tgt", None, None),
        P("rep", "src", "tgt", None),
        P("rep", "src", "tgt", None),
        P("rep", "src", "tgt"),
        P(),
        P(),
        P(),
        P(),
        P(),
    )
    sizes = tuple(mesh.shape[a] for a in AXES)
    return jax.shard_map(
        functools.partial(local, sizes),
        mesh=mesh,
        in_specs=placed,
        out_specs=(
            P("rep", ("src", "tgt"), None),
            P("src", None),
            P("src", None),
            P("src", None),
            P("src", None),
            P("src", None),
        ),
        check_vma=False,
    )
```

```python
import functools

import jax
import jax.numpy as jnp
from jax import lax
from jax.experimental import pallas as pl
from jax.experimental.pallas import tpu as pltpu
from jax.sharding import PartitionSpec as P

OFFSETS = (0, 1, 10, 35, 70)
ROT = 115
LANES = 128
STRIP = 32
AXES = ("rep", "src", "tgt")
F32 = jnp.float32
BF16 = jnp.bfloat16

GROUPS = (5, 4, 4, 3, 3)
STARTS = (0, 5, 9, 13, 16)


def place(level, order):
    group = {0: 0, 1: 1, -1: 2, 2: 3, -2: 4}[order]
    return STARTS[group] + level - abs(order)


def split(value):
    high = value.astype(BF16)
    return high, (value - high.astype(F32)).astype(BF16)


def nt(left, right):
    return lax.dot_general(left, right, (((1,), (1,)), ((), ())), preferred_element_type=F32)


def tn(left, right):
    return lax.dot_general(left, right, (((0,), (0,)), ((), ())), preferred_element_type=F32)


def nn(left, right):
    return lax.dot_general(left, right, (((1,), (0,)), ((), ())), preferred_element_type=F32)


def onehot(row, atoms, shard, mine, flip, twice=True):
    ids = row.astype(jnp.int32)
    bits = shard.bit_length() - 1
    rel = lax.shift_right_arithmetic(ids, bits) ^ mine
    if flip is not None:
        pair = rel & 3
        swapped = lax.shift_right_logical(pair, 1) | lax.shift_left(pair & 1, 1)
        rel = jnp.where(flip != 0, (rel & ~3) | swapped, rel)
    where = jnp.where(ids < 0, -1, lax.shift_left(rel, bits) | (ids & (shard - 1)))
    hit = lax.broadcasted_iota(jnp.int32, (atoms, row.shape[1]), 0) == where
    one = jnp.where(hit, 1.0, 0.0).astype(BF16)
    return jnp.concatenate([one, one], 0) if twice else one


def gather(shards, select, out, chans):
    for level in range(5):
        first, last = level * level * chans, (level + 1) * (level + 1) * chans
        rows = jnp.concatenate([s[:, first:last] for s in shards], 0)
        high, low = split(rows)
        out[first:last, :] = tn(jnp.concatenate([high, low], 0), select)


def spread(pack, out):
    tiles = out.shape[2] // LANES
    for k in range(ROT):
        for t in range(tiles):
            row = pack[k * tiles + t : k * tiles + t + 1, :]
            out[k, :, t * LANES : (t + 1) * LANES] = jnp.broadcast_to(row, (8, LANES))


def ends(pack, which, edges):
    tiles = edges // LANES
    at = (ROT + which) * tiles
    return jnp.concatenate([pack[at + t : at + t + 1, :] for t in range(tiles)], 1)


def prepare_kernel(count, rotation_any, source_any, target_any, pack, rotation, source, target, sems):
    pairs = ((rotation_any, rotation), (source_any, source), (target_any, target))
    copies = [pltpu.make_async_copy(a, b, sems.at[k]) for k, (a, b) in enumerate(pairs)]
    for copy in copies:
        copy.start()
    for copy in copies:
        copy.wait()
    rows, edges = rotation.shape[2], rotation.shape[4]
    tiles = edges // LANES
    for k in range(rows):
        for t in range(tiles):
            at = k * tiles + t
            pack[at : at + 1, :] = rotation[0, 0, k, :, t * LANES : (t + 1) * LANES]
    slot = lax.broadcasted_iota(jnp.int32, (1, LANES), 1)
    for which, end in enumerate((source, target)):
        for t in range(tiles):
            at = (rows + which) * tiles + t
            value = end[0, 0, :, t * LANES : (t + 1) * LANES]
            pack[at : at + 1, :] = jnp.where(slot + t * LANES < count[0, 0, 0], value, -1).astype(F32)
    at = (rows + 2) * tiles
    pack[at:, :] = jnp.zeros((pack.shape[0] - at, LANES), F32)


def rotate(rot, feats, base, store, chans):
    edges = rot.shape[2]
    tiles = edges // LANES

    def body(step, carry):
        tile = step % tiles
        strip = step // tiles
        lanes = pl.ds(pl.multiple_of(tile * LANES, LANES), LANES)
        wide = pl.ds(pl.multiple_of(base + tile * LANES, LANES), LANES)
        for level in range(5):
            order = min(level, 2)
            cols = 2 * level + 1
            acc = [[None] * (STRIP // 8) for _ in range(2 * order + 1)]
            for c in range(cols):
                row = pl.multiple_of((level * level + c) * chans + strip * STRIP, STRIP)
                x = feats[pl.ds(row, STRIP), wide]
                for r in range(2 * order + 1):
                    factor = rot[OFFSETS[level] + r * cols + c, :, lanes]
                    for part in range(STRIP // 8):
                        term = factor * x[part * 8 : part * 8 + 8]
                        acc[r][part] = term if c == 0 else acc[r][part] + term
            for r in range(2 * order + 1):
                store(place(level, r - order), strip, wide, jnp.concatenate(acc[r], 0))
        return carry

    lax.fori_loop(0, (chans // STRIP) * tiles, body, 0)


def source_kernel(count, shard, own_slots, chans, me, *refs):
    shards = refs[:count]
    pack = refs[count]
    high_out, low_out, feats, rot, picked = refs[count + 1 :]
    edges = rot.shape[2]
    tiles = edges // LANES
    rows = tuple(g * chans // (2 * own_slots) for g in GROUPS)
    bases = tuple(sum(GROUPS[:g]) * chans // 2 for g in range(5))
    select = onehot(ends(pack, 0, edges), count * shard, shard, me[1], None)
    gather(shards, select, feats, chans)
    spread(pack, rot)
    parts = STRIP // 8
    high = lax.shift_right_logical(me[0], 1)

    def pick(parity):
        for strip in range(chans // STRIP):

            def body(tile, carry):
                lanes = pl.ds(pl.multiple_of(tile * LANES, LANES), LANES)
                for level in range(5):
                    order = min(level, 2)
                    cols = 2 * level + 1
                    wanted = []
                    for r in range(2 * order + 1):
                        group = (0, 1, 3)[abs(r - order)] + (1 if r < order else 0)
                        for part in range(parts):
                            row = (level - abs(r - order)) * chans + strip * STRIP + part * 8
                            owner, inner = divmod(row, rows[group])
                            if owner % 2 == parity:
                                wanted.append((r, part, group, owner // 2, inner))
                    acc = {}
                    for c in range(cols if wanted else 0):
                        row = (level * level + c) * chans + strip * STRIP
                        x = feats[row : row + STRIP, lanes]
                        for r in sorted({w[0] for w in wanted}):
                            factor = rot[OFFSETS[level] + r * cols + c, :, lanes]
                            for part in (w[1] for w in wanted if w[0] == r):
                                term = factor * x[part * 8 : part * 8 + 8]
                                acc[r, part] = acc[r, part] + term if c else term
                    for r, part, group, slot, inner in wanted:
                        at = bases[group] + (slot ^ high) * rows[group] + inner
                        picked[pl.ds(pl.multiple_of(at, 8), 8), lanes] = acc[r, part]
                return carry

            lax.fori_loop(0, tiles, body, 0)

    for parity in range(2):
        pl.when((me[0] & 1) == parity)(functools.partial(pick, parity))
    high_out[...], low_out[...] = split(picked[...])


def weight_kernel(count, shard, own_slots, parts, chans, me, *refs):
    shards = refs[:count]
    packs = refs[count : count + 2]
    z_any = refs[count + 2 : count + 6]
    keep_any, send_any = refs[count + 6 : count + 8]
    u_any = refs[count + 8 : count + 14]
    feats, rot, zh, zl, uh, ul, full, load_sem, u_sem, out_sem = refs[count + 14 :]
    edges = rot.shape[2]
    owner, core, tgt = me[0], me[2], me[1]
    loads = [
        pltpu.make_async_copy(z, half.at[:, tile * edges : (tile + 1) * edges], load_sem.at[k])
        for k, (z, half, tile) in enumerate(zip(z_any, (zh, zl, zh, zl), (0, 0, 1, 1)))
    ]
    for load in loads:
        load.start()
    select = jnp.concatenate(
        [onehot(ends(p, 1, edges), count * shard, shard, owner, core) for p in packs], 1
    )
    gather(shards, select, feats, chans)

    def store(where, strip, lanes, value):
        high, low = split(value)
        rows = pl.ds(pl.multiple_of(where * chans + strip * STRIP, STRIP), STRIP)
        uh[rows, lanes] = high
        ul[rows, lanes] = low

    for tile in range(2):
        spread(packs[tile], rot)
        rotate(rot, feats, tile * edges, store, chans)
        if tile == 0:
            saves = []
            for k, first, last in ((0, 0, 5), (1, 5, 13), (2, 13, 19)):
                for j, half in ((0, uh), (1, ul)):
                    piece = half.at[first * chans : last * chans, 0:edges]
                    at = 2 * k + j
                    saves.append(pltpu.make_async_copy(piece, u_any[at], u_sem.at[at]))
            for save in saves:
                save.start()
    for load in loads:
        load.wait()

    def product(*terms):
        left, right = [], []
        for a, b in ((zh, uh), (zh, ul), (zl, uh)):
            for sign, z, u in terms:
                first = sum(GROUPS[:z]) * chans // 2
                value = a[first : first + GROUPS[z] * chans // 2, :]
                left.append(value if sign > 0 else -value)
                right.append(b[STARTS[u] * chans : (STARTS[u] + GROUPS[u]) * chans, :])
        return nt(jnp.concatenate(left, 1), jnp.concatenate(right, 1))

    def put(at, value):
        wide = value.shape[1] // LANES
        high = value.shape[0] // own_slots // 8
        for col in range(wide):
            block = value[:, col * LANES : (col + 1) * LANES]
            full[:, at + col * high : at + (col + 1) * high] = block.reshape(own_slots, high, 8, LANES)
        return at + wide * high

    at = put(0, product((1, 0, 0)))
    at = put(at, product((1, 1, 1), (1, 2, 2)))
    at = put(at, product((1, 1, 2), (-1, 2, 1)))
    at = put(at, product((1, 3, 3), (1, 4, 4)))
    at = put(at, product((1, 3, 4), (-1, 4, 3)))
    total = full.shape[1]
    if at < total:
        full[:, at:total] = jnp.zeros((own_slots, total - at, 8, LANES), F32)
    piece = total // (2 * parts)
    rest = parts * own_slots // 4
    copies = []
    for side, target in ((0, keep_any), (1, send_any)):
        for part in range(parts):
            for slot in range(own_slots):
                first, second = part & 1, slot & 1
                lower = (part >> 1) * (own_slots // 2) + (slot >> 1)
                pos = jnp.where(core == side, first * 2 + second, second * 2 + first) * rest + lower
                begin = ((core ^ side) * parts + (tgt ^ part)) * piece
                copy = pltpu.make_async_copy(
                    full.at[slot, pl.ds(begin, piece)], target.at[pos], out_sem.at[len(copies)]
                )
                copy.start()
                copies.append(copy)
    for copy in copies + saves:
        copy.wait()


def back_zero_kernel(w, uh, ul, out):
    wh, wl = split(w[...])
    high, low = uh[...], ul[...]
    out[...] = nn(jnp.concatenate([wh, wh, wl], 1), jnp.concatenate([high, low, high], 0))


def back_pair_kernel(re, im, uh, ul, out):
    size = re.shape[0]
    rh, rl = split(re[...])
    ih, il = split(im[...])
    ph, mh = uh[0:size, :], uh[size : 2 * size, :]
    pl_, ml = ul[0:size, :], ul[size : 2 * size, :]
    w = jnp.concatenate([rh, ih, rh, ih, rl, il], 1)
    out[0:size, :] = nn(w, jnp.concatenate([ph, mh, pl_, ml, ph, mh], 0))
    out[size : 2 * size, :] = nn(w, jnp.concatenate([mh, -ph, ml, -pl_, mh, -ph], 0))


def scatter_kernel(count, shard, chans, me, pack, d0, d1, d2, out, rot, back):
    edges = rot.shape[2]
    select = onehot(ends(pack, 0, edges), count * shard, shard, me[1], None, False)
    select = jnp.concatenate([select, select], 1)
    spread(pack, rot)
    tiles = edges // LANES
    pieces = (d0, d1, d2)
    firsts = (0, 5, 13)

    def load(where, strip, lanes):
        which = 0 if where < 5 else 1 if where < 13 else 2
        row = pl.multiple_of((where - firsts[which]) * chans + strip * 16, 16)
        return pieces[which][pl.ds(row, 16), lanes]

    def body(step, carry):
        tile = step % tiles
        strip = step // tiles
        lanes = pl.ds(pl.multiple_of(tile * LANES, LANES), LANES)
        for level in range(5):
            order = min(level, 2)
            cols = 2 * level + 1
            d = [load(place(level, r - order), strip, lanes) for r in range(2 * order + 1)]
            for c in range(cols):
                acc = [None, None]
                for r in range(2 * order + 1):
                    factor = rot[OFFSETS[level] + r * cols + c, :, lanes]
                    for half in range(2):
                        term = factor * d[r][half * 8 : half * 8 + 8]
                        acc[half] = term if r == 0 else acc[half] + term
                row = pl.multiple_of((level * level + c) * chans + strip * 16, 16)
                back[pl.ds(row, 16), lanes] = jnp.concatenate(acc, 0)
        return carry

    lax.fori_loop(0, (chans // 16) * tiles, body, 0)
    for level in range(5):
        first, last = level * level * chans, (level + 1) * (level + 1) * chans
        high, low = split(back[first:last, :])
        total = nt(select, jnp.concatenate([high, low], 1))
        for part in range(count):
            out[part, :, first:last] = total[part * shard : (part + 1) * shard]


def unpack_kernel(parts, chans, me, *refs):
    mine = refs[:parts]
    other = refs[parts : 2 * parts]
    outs = refs[2 * parts : 2 * parts + 5]
    tiles = refs[2 * parts + 5]
    piece = mine[0].shape[0]
    tgt, core = me[1], me[2]
    for side, group in ((0, mine), (1, other)):
        for part in range(parts):
            begin = ((core ^ side) * parts + (tgt ^ part)) * piece
            tiles[pl.ds(begin, piece)] = group[part][...]
    at = 0
    for out in outs:
        high, wide = out.shape[0] // 8, out.shape[1] // LANES
        for col in range(wide):
            block = tiles[at : at + high].reshape(high * 8, LANES)
            out[:, col * LANES : (col + 1) * LANES] = block
            at += high


def vmem(count):
    return [pl.BlockSpec(memory_space=pltpu.VMEM)] * count


def anywhere(count):
    return [pl.BlockSpec(memory_space=pl.ANY)] * count


SMEM = [pl.BlockSpec(memory_space=pltpu.SMEM)]


def call(kernel, name, ins, outs, shapes, scratch, micros, limit):
    return pl.pallas_call(
        kernel,
        name=name,
        in_specs=ins,
        out_specs=outs,
        out_shape=shapes,
        scratch_shapes=scratch,
        compiler_params=pltpu.CompilerParams(vmem_limit_bytes=limit * 1024 * 1024),
        cost_estimate=pl.CostEstimate(
            flops=int(micros * 1_150_000_000), bytes_accessed=100_000, transcendentals=0
        ),
    )


def shape(*dims, dtype=F32):
    return jax.ShapeDtypeStruct(dims, dtype)


def local(
    sizes,
    src_feats,
    tgt_cotangent,
    rotation,
    edge_src,
    edge_tgt,
    edge_count,
    w_zero,
    w_one_re,
    w_one_im,
    w_two_re,
    w_two_im,
):
    reps, nsrc, ntgt = sizes
    chans = w_zero.shape[0] // 5
    shard, feat = src_feats.shape[1], src_feats.shape[2]
    edges = edge_src.shape[-1]
    slots = nsrc // 2
    src_bits = nsrc.bit_length() - 1
    tgt_bits = ntgt.bit_length() - 1
    me_src, me_tgt, me_rep = (lax.axis_index(a).astype(jnp.int32) for a in ("src", "tgt", "rep"))
    me = jnp.stack([me_src, me_tgt, me_rep])

    def hop(value, axes, *routes):
        pairs = []
        for rep in range(reps):
            s_mask, t_mask = routes[rep % len(routes)]
            for s in range(nsrc):
                for t in range(ntgt):
                    base = rep * nsrc * ntgt
                    pairs.append((base + s * ntgt + t, base + (s ^ s_mask) * ntgt + (t ^ t_mask)))
        return lax.ppermute(value, AXES, pairs)

    def cross(value):
        half = nsrc * ntgt
        return lax.ppermute(value, AXES, [(i, (i + half) % (2 * half)) for i in range(2 * half)])

    tiles = edges // LANES
    length = -(-(ROT + 2) * tiles // 8) * 8
    pack = call(
        prepare_kernel,
        "prepare",
        SMEM + [pl.BlockSpec(memory_space=pltpu.HBM)] * 3,
        vmem(1)[0],
        shape(length, LANES),
        [
            pltpu.VMEM((1, 1, ROT, 1, edges), F32),
            pltpu.VMEM((1, 1, 1, edges), jnp.int32),
            pltpu.VMEM((1, 1, 1, edges), jnp.int32),
            pltpu.SemaphoreType.DMA((3,)),
        ],
        2,
        4,
    )(edge_count, jnp.transpose(rotation, (0, 1, 3, 2, 4)), edge_src, edge_tgt)
    x_own = src_feats[0]
    g_parts = {0: tgt_cotangent[0]}
    for bit in range(src_bits - 1, 1, -1):
        for k, part in list(g_parts.items()):
            g_parts[k | (1 << bit)] = hop(part, None, (1 << bit, 0))
    far = [k for k in g_parts if k > 0]
    first, second = ((1, 0), (2, 0)), ((2, 0), (1, 0))
    g_parts[1] = hop(g_parts[0], None, *first)
    x_other = hop(x_own, None, (1, 0))
    x_parts = [x_own] + [hop(x_own, None, (0, t)) for t in range(1, ntgt)]
    g_parts[2] = hop(g_parts[0], None, *second)
    arrived = [g_parts[k] for k in far]
    pack_other = hop(pack, None, (1, 0))
    y_parts = [x_other] + [hop(x_other, None, (0, t)) for t in range(1, ntgt)]
    g_parts[3] = hop(g_parts[1], None, *second)
    for k, part in zip(far, arrived):
        g_parts[k] = part
        g_parts[k | 1] = hop(part, None, *first)
        g_parts[k | 2] = hop(part, None, *second)
    groups = sum(GROUPS) * chans
    z_rows = groups // 2

    def source_rows(parts, rows):
        return call(
            functools.partial(source_kernel, ntgt, shard, slots, chans),
            "source_rows",
            SMEM + vmem(ntgt + 1),
            vmem(2),
            [shape(z_rows, edges, dtype=BF16)] * 2,
            [
                pltpu.VMEM((feat, edges), F32),
                pltpu.VMEM((ROT, 8, edges), F32),
                pltpu.VMEM((z_rows, edges), F32),
            ],
            2.5,
            20,
        )(me, *parts, rows)

    z_own = list(source_rows(x_parts, pack))
    arrived = [g_parts[k | 1] for k in far]
    for k, part in zip(far, arrived):
        g_parts[k | 1] = part
        g_parts[k | 3] = hop(part, None, *second)
    z_other = source_rows(y_parts, pack_other)
    g_list = [g_parts[k] for k in range(nsrc)]

    per_slot = sum(
        (w.shape[0] // nsrc // 8) * (w.shape[1] // LANES)
        for w in (w_zero, w_one_re, w_one_im, w_two_re, w_two_im)
    )
    piece = -(-per_slot // (reps * ntgt))
    subs = ntgt * slots
    keep, send, *u = call(
        functools.partial(weight_kernel, nsrc, shard, slots, ntgt, chans),
        "weight_terms",
        SMEM + vmem(nsrc + 2) + anywhere(4),
        anywhere(8),
        [shape(subs, piece, 8, LANES)] * 2
        + [shape(k * chans, edges, dtype=BF16) for k in (5, 5, 8, 8, 6, 6)],
        [
            pltpu.VMEM((feat, 2 * edges), F32),
            pltpu.VMEM((ROT, 8, edges), F32),
            pltpu.VMEM((z_rows, 2 * edges), BF16),
            pltpu.VMEM((z_rows, 2 * edges), BF16),
            pltpu.VMEM((groups, 2 * edges), BF16),
            pltpu.VMEM((groups, 2 * edges), BF16),
            pltpu.VMEM((slots, piece * reps * ntgt, 8, LANES), F32),
            pltpu.SemaphoreType.DMA((4,)),
            pltpu.SemaphoreType.DMA((6,)),
            pltpu.SemaphoreType.DMA((2 * subs,)),
        ],
        14,
        44,
    )(me, *g_list, pack, pack_other, *z_own, *z_other)

    d0 = call(
        back_zero_kernel, "back_zero", vmem(3), vmem(1)[0], shape(5 * chans, edges), [], 3, 20
    )(w_zero, *u[0:2])
    d1 = call(
        back_pair_kernel, "back_one", vmem(4), vmem(1)[0], shape(8 * chans, edges), [], 4, 24
    )(w_one_re, w_one_im, *u[2:4])
    d2 = call(
        back_pair_kernel, "back_two", vmem(4), vmem(1)[0], shape(6 * chans, edges), [], 3, 20
    )(w_two_re, w_two_im, *u[4:6])
    routes = [((0, 1), (2, 0)), ((2, 0), (0, 1))]
    routes += [((0, 1 << b),) * 2 for b in range(tgt_bits - 1, 0, -1)]
    routes += [((1 << b, 0),) * 2 for b in range(src_bits - 1, 1, -1)]
    held, came = keep, cross(send)
    for k, route in enumerate(routes):
        half = held.shape[0] // 2
        sent = held[half:] + came[half:]
        if k == 1:
            sent, d0, d1, d2 = lax.optimization_barrier((sent, d0, d1, d2))
            atoms = call(
                functools.partial(scatter_kernel, ntgt, shard, chans),
                "source_sums",
                SMEM + vmem(4),
                vmem(1)[0],
                shape(ntgt, shard, feat),
                [pltpu.VMEM((ROT, 8, edges), F32), pltpu.VMEM((feat, edges), F32)],
                5,
                24,
            )(me, pack, d0, d1, d2)
        if k == 2:
            sent, atoms = lax.optimization_barrier((sent, atoms))
        held = held[:half] + came[:half]
        came = hop(sent, None, *route)
    final = held[0] + came[0]

    for b in range(tgt_bits - 1, -1, -1):
        half = atoms.shape[0] // 2
        atoms = atoms[:half] + hop(atoms[half:], None, (0, 1 << b))
    grad_feats = atoms

    mine = [final] + [hop(final, None, (0, t)) for t in range(1, ntgt)]
    other = [cross(m) for m in mine]
    outs = call(
        functools.partial(unpack_kernel, ntgt, chans),
        "unpack",
        SMEM + vmem(2 * ntgt),
        vmem(5),
        [
            shape(w.shape[0] // nsrc, w.shape[1])
            for w in (w_zero, w_one_re, w_one_im, w_two_re, w_two_im)
        ],
        [pltpu.VMEM((piece * reps * ntgt, 8, LANES), F32)],
        2,
        8,
    )(me, *mine, *other)
    return (grad_feats, *outs)


def solution(mesh):
    placed = (
        P("rep", ("src", "tgt"), None),
        P("rep", ("tgt", "src"), None),
        P("rep", "src", "tgt", None, None),
        P("rep", "src", "tgt", None),
        P("rep", "src", "tgt", None),
        P("rep", "src", "tgt"),
        P(),
        P(),
        P(),
        P(),
        P(),
    )
    sizes = tuple(mesh.shape[a] for a in AXES)
    return jax.shard_map(
        functools.partial(local, sizes),
        mesh=mesh,
        in_specs=placed,
        out_specs=(
            P("rep", ("src", "tgt"), None),
            P("src", None),
            P("src", None),
            P("src", None),
            P("src", None),
            P("src", None),
        ),
        check_vma=False,
    )
```

```python
import functools

import jax
import jax.numpy as jnp
from jax import lax
from jax.experimental import pallas as pl
from jax.experimental.pallas import tpu as pltpu
from jax.sharding import PartitionSpec as P

OFFSETS = (0, 1, 10, 35, 70)
ROT = 115
LANES = 128
STRIP = 32
AXES = ("rep", "src", "tgt")
F32 = jnp.float32
BF16 = jnp.bfloat16

GROUPS = (5, 4, 4, 3, 3)
STARTS = (0, 5, 9, 13, 16)


def place(level, order):
    group = {0: 0, 1: 1, -1: 2, 2: 3, -2: 4}[order]
    return STARTS[group] + level - abs(order)


def split(value):
    high = value.astype(BF16)
    return high, (value - high.astype(F32)).astype(BF16)


def nt(left, right):
    return lax.dot_general(left, right, (((1,), (1,)), ((), ())), preferred_element_type=F32)


def tn(left, right):
    return lax.dot_general(left, right, (((0,), (0,)), ((), ())), preferred_element_type=F32)


def nn(left, right):
    return lax.dot_general(left, right, (((1,), (0,)), ((), ())), preferred_element_type=F32)


def twist(index, top):
    return index ^ lax.shift_left(lax.shift_right_logical(index, top) & 1, top - 1)


def onehot(row, atoms, shard, mine, top=None, flip=None, twice=True):
    ids = row.astype(jnp.int32)
    bits = shard.bit_length() - 1
    rel = lax.shift_right_arithmetic(ids, bits) ^ mine
    if top is not None:
        rel = twist(rel, top)
        differ = (rel ^ lax.shift_right_logical(rel, 1)) & 1
        rel = jnp.where(flip != 0, rel ^ (differ * 3), rel)
    where = jnp.where(ids < 0, -1, lax.shift_left(rel, bits) | (ids & (shard - 1)))
    hit = lax.broadcasted_iota(jnp.int32, (atoms, row.shape[1]), 0) == where
    one = jnp.where(hit, 1.0, 0.0).astype(BF16)
    return jnp.concatenate([one, one], 0) if twice else one


def gather(shards, select, out, chans):
    for level in range(5):
        first, last = level * level * chans, (level + 1) * (level + 1) * chans
        rows = jnp.concatenate([s[:, first:last] for s in shards], 0)
        high, low = split(rows)
        out[first:last, :] = tn(jnp.concatenate([high, low], 0), select)


def spread(pack, out):
    tiles = out.shape[2] // LANES
    for k in range(ROT):
        for t in range(tiles):
            row = pack[k * tiles + t : k * tiles + t + 1, :]
            out[k, :, t * LANES : (t + 1) * LANES] = jnp.broadcast_to(row, (8, LANES))


def ends(pack, which, edges):
    tiles = edges // LANES
    at = (ROT + which) * tiles
    return jnp.concatenate([pack[at + t : at + t + 1, :] for t in range(tiles)], 1)


def prepare_kernel(count, rotation_any, source_any, target_any, pack, rotation, source, target, sems):
    pairs = ((rotation_any, rotation), (source_any, source), (target_any, target))
    copies = [pltpu.make_async_copy(a, b, sems.at[k]) for k, (a, b) in enumerate(pairs)]
    for copy in copies:
        copy.start()
    for copy in copies:
        copy.wait()
    rows, edges = rotation.shape[2], rotation.shape[4]
    tiles = edges // LANES
    for k in range(rows):
        for t in range(tiles):
            at = k * tiles + t
            pack[at : at + 1, :] = rotation[0, 0, k, :, t * LANES : (t + 1) * LANES]
    slot = lax.broadcasted_iota(jnp.int32, (1, LANES), 1)
    for which, end in enumerate((source, target)):
        for t in range(tiles):
            at = (rows + which) * tiles + t
            value = end[0, 0, :, t * LANES : (t + 1) * LANES]
            pack[at : at + 1, :] = jnp.where(slot + t * LANES < count[0, 0, 0], value, -1).astype(F32)
    at = (rows + 2) * tiles
    pack[at:, :] = jnp.zeros((pack.shape[0] - at, LANES), F32)


def rotate(rot, feats, base, store, chans):
    edges = rot.shape[2]
    tiles = edges // LANES

    def body(step, carry):
        tile = step % tiles
        strip = step // tiles
        lanes = pl.ds(pl.multiple_of(tile * LANES, LANES), LANES)
        wide = pl.ds(pl.multiple_of(base + tile * LANES, LANES), LANES)
        for level in range(5):
            order = min(level, 2)
            cols = 2 * level + 1
            acc = [[None] * (STRIP // 8) for _ in range(2 * order + 1)]
            for c in range(cols):
                row = pl.multiple_of((level * level + c) * chans + strip * STRIP, STRIP)
                x = feats[pl.ds(row, STRIP), wide]
                for r in range(2 * order + 1):
                    factor = rot[OFFSETS[level] + r * cols + c, :, lanes]
                    for part in range(STRIP // 8):
                        term = factor * x[part * 8 : part * 8 + 8]
                        acc[r][part] = term if c == 0 else acc[r][part] + term
            for r in range(2 * order + 1):
                store(place(level, r - order), strip, wide, jnp.concatenate(acc[r], 0))
        return carry

    lax.fori_loop(0, (chans // STRIP) * tiles, body, 0)


def source_kernel(count, shard, own_slots, chans, me, *refs):
    shards = refs[:count]
    pack = refs[count]
    high_out, low_out, feats, rot, picked = refs[count + 1 :]
    edges = rot.shape[2]
    tiles = edges // LANES
    rows = tuple(g * chans // (2 * own_slots) for g in GROUPS)
    bases = tuple(sum(GROUPS[:g]) * chans // 2 for g in range(5))
    select = onehot(ends(pack, 0, edges), count * shard, shard, me[1])
    gather(shards, select, feats, chans)
    spread(pack, rot)
    parts = STRIP // 8
    high = lax.shift_right_logical(me[0], 1)
    top = own_slots.bit_length() - 2

    def pick(parity):
        for strip in range(chans // STRIP):

            def body(tile, carry):
                lanes = pl.ds(pl.multiple_of(tile * LANES, LANES), LANES)
                for level in range(5):
                    order = min(level, 2)
                    cols = 2 * level + 1
                    wanted = []
                    for r in range(2 * order + 1):
                        group = (0, 1, 3)[abs(r - order)] + (1 if r < order else 0)
                        for part in range(parts):
                            row = (level - abs(r - order)) * chans + strip * STRIP + part * 8
                            owner, inner = divmod(row, rows[group])
                            if owner % 2 == parity:
                                wanted.append((r, part, group, owner // 2, inner))
                    acc = {}
                    for c in range(cols if wanted else 0):
                        row = (level * level + c) * chans + strip * STRIP
                        x = feats[row : row + STRIP, lanes]
                        for r in sorted({w[0] for w in wanted}):
                            factor = rot[OFFSETS[level] + r * cols + c, :, lanes]
                            for part in (w[1] for w in wanted if w[0] == r):
                                term = factor * x[part * 8 : part * 8 + 8]
                                acc[r, part] = acc[r, part] + term if c else term
                    for r, part, group, slot, inner in wanted:
                        at = bases[group] + twist(slot ^ high, top) * rows[group] + inner
                        picked[pl.ds(pl.multiple_of(at, 8), 8), lanes] = acc[r, part]
                return carry

            lax.fori_loop(0, tiles, body, 0)

    for parity in range(2):
        pl.when((me[0] & 1) == parity)(functools.partial(pick, parity))
    high_out[...], low_out[...] = split(picked[...])


def weight_kernel(count, shard, own_slots, parts, chans, me, *refs):
    shards = refs[:count]
    packs = refs[count : count + 2]
    z_any = refs[count + 2 : count + 6]
    keep_any, send_any = refs[count + 6 : count + 8]
    u_any = refs[count + 8 : count + 14]
    feats, rot, zh, zl, uh, ul, full, load_sem, u_sem, out_sem = refs[count + 14 :]
    edges = rot.shape[2]
    owner, core, tgt = me[0], me[2], me[1]
    loads = [
        pltpu.make_async_copy(z, half.at[:, tile * edges : (tile + 1) * edges], load_sem.at[k])
        for k, (z, half, tile) in enumerate(zip(z_any, (zh, zl, zh, zl), (0, 0, 1, 1)))
    ]
    for load in loads:
        load.start()
    select = jnp.concatenate(
        [onehot(ends(p, 1, edges), count * shard, shard, owner, own_slots.bit_length() - 1, core) for p in packs], 1
    )
    gather(shards, select, feats, chans)

    def store(where, strip, lanes, value):
        high, low = split(value)
        rows = pl.ds(pl.multiple_of(where * chans + strip * STRIP, STRIP), STRIP)
        uh[rows, lanes] = high
        ul[rows, lanes] = low

    for tile in range(2):
        spread(packs[tile], rot)
        rotate(rot, feats, tile * edges, store, chans)
        if tile == 0:
            saves = []
            for k, first, last in ((0, 0, 5), (1, 5, 13), (2, 13, 19)):
                for j, half in ((0, uh), (1, ul)):
                    piece = half.at[first * chans : last * chans, 0:edges]
                    at = 2 * k + j
                    saves.append(pltpu.make_async_copy(piece, u_any[at], u_sem.at[at]))
            for save in saves:
                save.start()
    for load in loads:
        load.wait()

    def product(*terms):
        left, right = [], []
        for a, b in ((zh, uh), (zh, ul), (zl, uh)):
            for sign, z, u in terms:
                first = sum(GROUPS[:z]) * chans // 2
                value = a[first : first + GROUPS[z] * chans // 2, :]
                left.append(value if sign > 0 else -value)
                right.append(b[STARTS[u] * chans : (STARTS[u] + GROUPS[u]) * chans, :])
        return nt(jnp.concatenate(left, 1), jnp.concatenate(right, 1))

    def put(at, value):
        wide = value.shape[1] // LANES
        high = value.shape[0] // own_slots // 8
        for col in range(wide):
            block = value[:, col * LANES : (col + 1) * LANES]
            full[:, at + col * high : at + (col + 1) * high] = block.reshape(own_slots, high, 8, LANES)
        return at + wide * high

    at = put(0, product((1, 0, 0)))
    at = put(at, product((1, 1, 1), (1, 2, 2)))
    at = put(at, product((1, 1, 2), (-1, 2, 1)))
    at = put(at, product((1, 3, 3), (1, 4, 4)))
    at = put(at, product((1, 3, 4), (-1, 4, 3)))
    total = full.shape[1]
    if at < total:
        full[:, at:total] = jnp.zeros((own_slots, total - at, 8, LANES), F32)
    piece = total // (2 * parts)
    rest = parts * own_slots // 4
    copies = []
    for side, target in ((0, keep_any), (1, send_any)):
        for part in range(parts):
            for slot in range(own_slots):
                first, second = part & 1, slot & 1
                lower = (part >> 1) * (own_slots // 2) + (slot >> 1)
                pos = jnp.where(core == side, first * 2 + second, second * 2 + first) * rest + lower
                begin = ((core ^ side) * parts + (tgt ^ part)) * piece
                copy = pltpu.make_async_copy(
                    full.at[slot, pl.ds(begin, piece)], target.at[pos], out_sem.at[len(copies)]
                )
                copy.start()
                copies.append(copy)
    for copy in copies + saves:
        copy.wait()


def back_zero_kernel(w, uh, ul, out):
    wh, wl = split(w[...])
    high, low = uh[...], ul[...]
    out[...] = nn(jnp.concatenate([wh, wh, wl], 1), jnp.concatenate([high, low, high], 0))


def back_pair_kernel(re, im, uh, ul, out):
    size = re.shape[0]
    rh, rl = split(re[...])
    ih, il = split(im[...])
    ph, mh = uh[0:size, :], uh[size : 2 * size, :]
    pl_, ml = ul[0:size, :], ul[size : 2 * size, :]
    w = jnp.concatenate([rh, ih, rh, ih, rl, il], 1)
    out[0:size, :] = nn(w, jnp.concatenate([ph, mh, pl_, ml, ph, mh], 0))
    out[size : 2 * size, :] = nn(w, jnp.concatenate([mh, -ph, ml, -pl_, mh, -ph], 0))


def scatter_kernel(count, shard, chans, me, pack, d0, d1, d2, out, rot, back):
    edges = rot.shape[2]
    select = onehot(ends(pack, 0, edges), count * shard, shard, me[1], twice=False)
    select = jnp.concatenate([select, select], 1)
    spread(pack, rot)
    tiles = edges // LANES
    pieces = (d0, d1, d2)
    firsts = (0, 5, 13)

    def load(where, strip, lanes):
        which = 0 if where < 5 else 1 if where < 13 else 2
        row = pl.multiple_of((where - firsts[which]) * chans + strip * 16, 16)
        return pieces[which][pl.ds(row, 16), lanes]

    def body(step, carry):
        tile = step % tiles
        strip = step // tiles
        lanes = pl.ds(pl.multiple_of(tile * LANES, LANES), LANES)
        for level in range(5):
            order = min(level, 2)
            cols = 2 * level + 1
            d = [load(place(level, r - order), strip, lanes) for r in range(2 * order + 1)]
            for c in range(cols):
                acc = [None, None]
                for r in range(2 * order + 1):
                    factor = rot[OFFSETS[level] + r * cols + c, :, lanes]
                    for half in range(2):
                        term = factor * d[r][half * 8 : half * 8 + 8]
                        acc[half] = term if r == 0 else acc[half] + term
                row = pl.multiple_of((level * level + c) * chans + strip * 16, 16)
                back[pl.ds(row, 16), lanes] = jnp.concatenate(acc, 0)
        return carry

    lax.fori_loop(0, (chans // 16) * tiles, body, 0)
    for level in range(5):
        first, last = level * level * chans, (level + 1) * (level + 1) * chans
        high, low = split(back[first:last, :])
        total = nt(select, jnp.concatenate([high, low], 1))
        for part in range(count):
            out[part, :, first:last] = total[part * shard : (part + 1) * shard]


def unpack_kernel(parts, chans, me, *refs):
    mine = refs[:parts]
    other = refs[parts : 2 * parts]
    outs = refs[2 * parts : 2 * parts + 5]
    tiles = refs[2 * parts + 5]
    piece = mine[0].shape[0]
    tgt, core = me[1], me[2]
    for side, group in ((0, mine), (1, other)):
        for part in range(parts):
            begin = ((core ^ side) * parts + (tgt ^ part)) * piece
            tiles[pl.ds(begin, piece)] = group[part][...]
    at = 0
    for out in outs:
        high, wide = out.shape[0] // 8, out.shape[1] // LANES
        for col in range(wide):
            block = tiles[at : at + high].reshape(high * 8, LANES)
            out[:, col * LANES : (col + 1) * LANES] = block
            at += high


def vmem(count):
    return [pl.BlockSpec(memory_space=pltpu.VMEM)] * count


def anywhere(count):
    return [pl.BlockSpec(memory_space=pl.ANY)] * count


SMEM = [pl.BlockSpec(memory_space=pltpu.SMEM)]


def call(kernel, name, ins, outs, shapes, scratch, micros, limit):
    return pl.pallas_call(
        kernel,
        name=name,
        in_specs=ins,
        out_specs=outs,
        out_shape=shapes,
        scratch_shapes=scratch,
        compiler_params=pltpu.CompilerParams(vmem_limit_bytes=limit * 1024 * 1024),
        cost_estimate=pl.CostEstimate(
            flops=int(micros * 1_150_000_000), bytes_accessed=100_000, transcendentals=0
        ),
    )


def shape(*dims, dtype=F32):
    return jax.ShapeDtypeStruct(dims, dtype)


def local(
    sizes,
    src_feats,
    tgt_cotangent,
    rotation,
    edge_src,
    edge_tgt,
    edge_count,
    w_zero,
    w_one_re,
    w_one_im,
    w_two_re,
    w_two_im,
):
    reps, nsrc, ntgt = sizes
    chans = w_zero.shape[0] // 5
    shard, feat = src_feats.shape[1], src_feats.shape[2]
    edges = edge_src.shape[-1]
    slots = nsrc // 2
    src_bits = nsrc.bit_length() - 1
    tgt_bits = ntgt.bit_length() - 1
    me_src, me_tgt, me_rep = (lax.axis_index(a).astype(jnp.int32) for a in ("src", "tgt", "rep"))
    me = jnp.stack([me_src, me_tgt, me_rep])

    def hop(value, axes, *routes):
        pairs = []
        for rep in range(reps):
            s_mask, t_mask = routes[rep % len(routes)]
            for s in range(nsrc):
                for t in range(ntgt):
                    base = rep * nsrc * ntgt
                    pairs.append((base + s * ntgt + t, base + (s ^ s_mask) * ntgt + (t ^ t_mask)))
        return lax.ppermute(value, AXES, pairs)

    def cross(value):
        half = nsrc * ntgt
        return lax.ppermute(value, AXES, [(i, (i + half) % (2 * half)) for i in range(2 * half)])

    tiles = edges // LANES
    length = -(-(ROT + 2) * tiles // 8) * 8
    pack = call(
        prepare_kernel,
        "prepare",
        SMEM + [pl.BlockSpec(memory_space=pltpu.HBM)] * 3,
        vmem(1)[0],
        shape(length, LANES),
        [
            pltpu.VMEM((1, 1, ROT, 1, edges), F32),
            pltpu.VMEM((1, 1, 1, edges), jnp.int32),
            pltpu.VMEM((1, 1, 1, edges), jnp.int32),
            pltpu.SemaphoreType.DMA((3,)),
        ],
        2,
        4,
    )(edge_count, jnp.transpose(rotation, (0, 1, 3, 2, 4)), edge_src, edge_tgt)
    x_own = src_feats[0]
    masks = [1 << b for b in range(src_bits)]
    masks[-1] |= masks[-2]
    g_parts = {0: tgt_cotangent[0]}
    for bit in range(src_bits - 1, 1, -1):
        for k, part in list(g_parts.items()):
            g_parts[k | (1 << bit)] = hop(part, None, (masks[bit], 0))
    far = [k for k in g_parts if k > 0]
    first, second = ((1, 0), (2, 0)), ((2, 0), (1, 0))
    g_parts[1] = hop(g_parts[0], None, *first)
    x_other = hop(x_own, None, (1, 0))
    x_parts = [x_own] + [hop(x_own, None, (0, t)) for t in range(1, ntgt)]
    g_parts[2] = hop(g_parts[0], None, *second)
    arrived = [g_parts[k] for k in far]
    pack_other = hop(pack, None, (1, 0))
    y_parts = [x_other] + [hop(x_other, None, (0, t)) for t in range(1, ntgt)]
    g_parts[3] = hop(g_parts[1], None, *second)
    for k, part in zip(far, arrived):
        g_parts[k] = part
        g_parts[k | 1] = hop(part, None, *first)
        g_parts[k | 2] = hop(part, None, *second)
    groups = sum(GROUPS) * chans
    z_rows = groups // 2

    def source_rows(parts, rows):
        return call(
            functools.partial(source_kernel, ntgt, shard, slots, chans),
            "source_rows",
            SMEM + vmem(ntgt + 1),
            vmem(2),
            [shape(z_rows, edges, dtype=BF16)] * 2,
            [
                pltpu.VMEM((feat, edges), F32),
                pltpu.VMEM((ROT, 8, edges), F32),
                pltpu.VMEM((z_rows, edges), F32),
            ],
            2.5,
            20,
        )(me, *parts, rows)

    z_own = list(source_rows(x_parts, pack))
    arrived = [g_parts[k | 1] for k in far]
    for k, part in zip(far, arrived):
        g_parts[k | 1] = part
        g_parts[k | 3] = hop(part, None, *second)
    z_other = source_rows(y_parts, pack_other)
    g_list = [g_parts[k] for k in range(nsrc)]

    per_slot = sum(
        (w.shape[0] // nsrc // 8) * (w.shape[1] // LANES)
        for w in (w_zero, w_one_re, w_one_im, w_two_re, w_two_im)
    )
    piece = -(-per_slot // (reps * ntgt))
    subs = ntgt * slots
    keep, send, *u = call(
        functools.partial(weight_kernel, nsrc, shard, slots, ntgt, chans),
        "weight_terms",
        SMEM + vmem(nsrc + 2) + anywhere(4),
        anywhere(8),
        [shape(subs, piece, 8, LANES)] * 2
        + [shape(k * chans, edges, dtype=BF16) for k in (5, 5, 8, 8, 6, 6)],
        [
            pltpu.VMEM((feat, 2 * edges), F32),
            pltpu.VMEM((ROT, 8, edges), F32),
            pltpu.VMEM((z_rows, 2 * edges), BF16),
            pltpu.VMEM((z_rows, 2 * edges), BF16),
            pltpu.VMEM((groups, 2 * edges), BF16),
            pltpu.VMEM((groups, 2 * edges), BF16),
            pltpu.VMEM((slots, piece * reps * ntgt, 8, LANES), F32),
            pltpu.SemaphoreType.DMA((4,)),
            pltpu.SemaphoreType.DMA((6,)),
            pltpu.SemaphoreType.DMA((2 * subs,)),
        ],
        14,
        44,
    )(me, *g_list, pack, pack_other, *z_own, *z_other)

    d0 = call(
        back_zero_kernel, "back_zero", vmem(3), vmem(1)[0], shape(5 * chans, edges), [], 3, 20
    )(w_zero, *u[0:2])
    d1 = call(
        back_pair_kernel, "back_one", vmem(4), vmem(1)[0], shape(8 * chans, edges), [], 4, 24
    )(w_one_re, w_one_im, *u[2:4])
    d2 = call(
        back_pair_kernel, "back_two", vmem(4), vmem(1)[0], shape(6 * chans, edges), [], 3, 20
    )(w_two_re, w_two_im, *u[4:6])
    routes = [((0, 1), (2, 0)), ((2, 0), (0, 1))]
    routes += [((0, 1 << b),) * 2 for b in range(tgt_bits - 1, 0, -1)]
    routes += [((masks[b], 0),) * 2 for b in range(src_bits - 1, 1, -1)]
    held, came = keep, cross(send)
    for k, route in enumerate(routes):
        half = held.shape[0] // 2
        sent = held[half:] + came[half:]
        if k == 1:
            sent, d0, d1, d2 = lax.optimization_barrier((sent, d0, d1, d2))
            atoms = call(
                functools.partial(scatter_kernel, ntgt, shard, chans),
                "source_sums",
                SMEM + vmem(4),
                vmem(1)[0],
                shape(ntgt, shard, feat),
                [pltpu.VMEM((ROT, 8, edges), F32), pltpu.VMEM((feat, edges), F32)],
                5,
                24,
            )(me, pack, d0, d1, d2)
        if k == 2:
            sent, atoms = lax.optimization_barrier((sent, atoms))
        held = held[:half] + came[:half]
        came = hop(sent, None, *route)
    final = held[0] + came[0]

    for b in range(tgt_bits - 1, -1, -1):
        half = atoms.shape[0] // 2
        atoms = atoms[:half] + hop(atoms[half:], None, (0, 1 << b))
    grad_feats = atoms

    mine = [final] + [hop(final, None, (0, t)) for t in range(1, ntgt)]
    other = [cross(m) for m in mine]
    outs = call(
        functools.partial(unpack_kernel, ntgt, chans),
        "unpack",
        SMEM + vmem(2 * ntgt),
        vmem(5),
        [
            shape(w.shape[0] // nsrc, w.shape[1])
            for w in (w_zero, w_one_re, w_one_im, w_two_re, w_two_im)
        ],
        [pltpu.VMEM((piece * reps * ntgt, 8, LANES), F32)],
        2,
        8,
    )(me, *mine, *other)
    return (grad_feats, *outs)


def solution(mesh):
    placed = (
        P("rep", ("src", "tgt"), None),
        P("rep", ("tgt", "src"), None),
        P("rep", "src", "tgt", None, None),
        P("rep", "src", "tgt", None),
        P("rep", "src", "tgt", None),
        P("rep", "src", "tgt"),
        P(),
        P(),
        P(),
        P(),
        P(),
    )
    sizes = tuple(mesh.shape[a] for a in AXES)
    return jax.shard_map(
        functools.partial(local, sizes),
        mesh=mesh,
        in_specs=placed,
        out_specs=(
            P("rep", ("src", "tgt"), None),
            P("src", None),
            P("src", None),
            P("src", None),
            P("src", None),
            P("src", None),
        ),
        check_vma=False,
    )
```

```python
import functools

import jax
import jax.numpy as jnp
from jax import lax
from jax.experimental import pallas as pl
from jax.experimental.pallas import tpu as pltpu
from jax.sharding import PartitionSpec as P

OFFSETS = (0, 1, 10, 35, 70)
ROT = 115
LANES = 128
STRIP = 64
AXES = ("rep", "src", "tgt")
F32 = jnp.float32
BF16 = jnp.bfloat16

GROUPS = (5, 4, 4, 3, 3)
STARTS = (0, 5, 9, 13, 16)


def place(level, order):
    group = {0: 0, 1: 1, -1: 2, 2: 3, -2: 4}[order]
    return STARTS[group] + level - abs(order)


def split(value):
    high = value.astype(BF16)
    return high, (value - high.astype(F32)).astype(BF16)


def nt(left, right):
    return lax.dot_general(left, right, (((1,), (1,)), ((), ())), preferred_element_type=F32)


def tn(left, right):
    return lax.dot_general(left, right, (((0,), (0,)), ((), ())), preferred_element_type=F32)


def nn(left, right):
    return lax.dot_general(left, right, (((1,), (0,)), ((), ())), preferred_element_type=F32)


def twist(index, top):
    return index ^ lax.shift_left(lax.shift_right_logical(index, top) & 1, top - 1)


def onehot(row, atoms, shard, mine, top=None, flip=None, twice=True):
    ids = row.astype(jnp.int32)
    bits = shard.bit_length() - 1
    rel = lax.shift_right_arithmetic(ids, bits) ^ mine
    if top is not None:
        rel = twist(rel, top)
        differ = (rel ^ lax.shift_right_logical(rel, 1)) & 1
        rel = jnp.where(flip != 0, rel ^ (differ * 3), rel)
    where = jnp.where(ids < 0, -1, lax.shift_left(rel, bits) | (ids & (shard - 1)))
    hit = lax.broadcasted_iota(jnp.int32, (atoms, row.shape[1]), 0) == where
    one = jnp.where(hit, 1.0, 0.0).astype(BF16)
    return jnp.concatenate([one, one], 0) if twice else one


def gather(shards, select, out, chans):
    for level in range(5):
        first, last = level * level * chans, (level + 1) * (level + 1) * chans
        rows = jnp.concatenate([s[:, first:last] for s in shards], 0)
        high, low = split(rows)
        out[first:last, :] = tn(jnp.concatenate([high, low], 0), select)


def spread(pack, out):
    tiles = out.shape[2] // LANES
    for k in range(ROT):
        for t in range(tiles):
            row = pack[k * tiles + t : k * tiles + t + 1, :]
            out[k, :, t * LANES : (t + 1) * LANES] = jnp.broadcast_to(row, (8, LANES))


def ends(pack, which, edges):
    tiles = edges // LANES
    at = (ROT + which) * tiles
    return jnp.concatenate([pack[at + t : at + t + 1, :] for t in range(tiles)], 1)


def prepare_kernel(count, rotation_any, source_any, target_any, pack, rotation, source, target, sems):
    pairs = ((rotation_any, rotation), (source_any, source), (target_any, target))
    copies = [pltpu.make_async_copy(a, b, sems.at[k]) for k, (a, b) in enumerate(pairs)]
    for copy in copies:
        copy.start()
    for copy in copies:
        copy.wait()
    rows, edges = rotation.shape[2], rotation.shape[4]
    tiles = edges // LANES
    for k in range(rows):
        for t in range(tiles):
            at = k * tiles + t
            pack[at : at + 1, :] = rotation[0, 0, k, :, t * LANES : (t + 1) * LANES]
    slot = lax.broadcasted_iota(jnp.int32, (1, LANES), 1)
    for which, end in enumerate((source, target)):
        for t in range(tiles):
            at = (rows + which) * tiles + t
            value = end[0, 0, :, t * LANES : (t + 1) * LANES]
            pack[at : at + 1, :] = jnp.where(slot + t * LANES < count[0, 0, 0], value, -1).astype(F32)
    at = (rows + 2) * tiles
    pack[at:, :] = jnp.zeros((pack.shape[0] - at, LANES), F32)


def rotate(rot, feats, base, store, chans):
    edges = rot.shape[2]
    tiles = edges // LANES

    def body(step, carry):
        tile = step % tiles
        strip = step // tiles
        lanes = pl.ds(pl.multiple_of(tile * LANES, LANES), LANES)
        wide = pl.ds(pl.multiple_of(base + tile * LANES, LANES), LANES)
        for level in range(5):
            order = min(level, 2)
            cols = 2 * level + 1
            acc = [[None] * (STRIP // 8) for _ in range(2 * order + 1)]
            for c in range(cols):
                row = pl.multiple_of((level * level + c) * chans + strip * STRIP, STRIP)
                x = feats[pl.ds(row, STRIP), wide]
                for r in range(2 * order + 1):
                    factor = rot[OFFSETS[level] + r * cols + c, :, lanes]
                    for part in range(STRIP // 8):
                        term = factor * x[part * 8 : part * 8 + 8]
                        acc[r][part] = term if c == 0 else acc[r][part] + term
            for r in range(2 * order + 1):
                store(place(level, r - order), strip, wide, jnp.concatenate(acc[r], 0))
        return carry

    lax.fori_loop(0, (chans // STRIP) * tiles, body, 0)


def source_kernel(count, shard, own_slots, chans, me, *refs):
    shards = refs[:count]
    pack = refs[count]
    high_out, low_out, feats, rot, picked = refs[count + 1 :]
    edges = rot.shape[2]
    tiles = edges // LANES
    rows = tuple(g * chans // (2 * own_slots) for g in GROUPS)
    bases = tuple(sum(GROUPS[:g]) * chans // 2 for g in range(5))
    select = onehot(ends(pack, 0, edges), count * shard, shard, me[1])
    gather(shards, select, feats, chans)
    spread(pack, rot)
    parts = STRIP // 8
    high = lax.shift_right_logical(me[0], 1)
    top = own_slots.bit_length() - 2

    def pick(parity):
        for strip in range(chans // STRIP):

            def body(tile, carry):
                lanes = pl.ds(pl.multiple_of(tile * LANES, LANES), LANES)
                for level in range(5):
                    order = min(level, 2)
                    cols = 2 * level + 1
                    wanted = []
                    for r in range(2 * order + 1):
                        group = (0, 1, 3)[abs(r - order)] + (1 if r < order else 0)
                        for part in range(parts):
                            row = (level - abs(r - order)) * chans + strip * STRIP + part * 8
                            owner, inner = divmod(row, rows[group])
                            if owner % 2 == parity:
                                wanted.append((r, part, group, owner // 2, inner))
                    acc = {}
                    for c in range(cols if wanted else 0):
                        row = (level * level + c) * chans + strip * STRIP
                        x = feats[row : row + STRIP, lanes]
                        for r in sorted({w[0] for w in wanted}):
                            factor = rot[OFFSETS[level] + r * cols + c, :, lanes]
                            for part in (w[1] for w in wanted if w[0] == r):
                                term = factor * x[part * 8 : part * 8 + 8]
                                acc[r, part] = acc[r, part] + term if c else term
                    for r, part, group, slot, inner in wanted:
                        at = bases[group] + twist(slot ^ high, top) * rows[group] + inner
                        picked[pl.ds(pl.multiple_of(at, 8), 8), lanes] = acc[r, part]
                return carry

            lax.fori_loop(0, tiles, body, 0)

    for parity in range(2):
        pl.when((me[0] & 1) == parity)(functools.partial(pick, parity))
    high_out[...], low_out[...] = split(picked[...])


def weight_kernel(count, shard, own_slots, parts, chans, me, *refs):
    shards = refs[:count]
    packs = refs[count : count + 2]
    z_any = refs[count + 2 : count + 6]
    keep_any, send_any = refs[count + 6 : count + 8]
    u_any = refs[count + 8 : count + 14]
    feats, rot, zh, zl, uh, ul, full, load_sem, u_sem, out_sem = refs[count + 14 :]
    edges = rot.shape[2]
    owner, core, tgt = me[0], me[2], me[1]
    loads = [
        pltpu.make_async_copy(z, half.at[:, tile * edges : (tile + 1) * edges], load_sem.at[k])
        for k, (z, half, tile) in enumerate(zip(z_any, (zh, zl, zh, zl), (0, 0, 1, 1)))
    ]
    for load in loads:
        load.start()
    select = jnp.concatenate(
        [onehot(ends(p, 1, edges), count * shard, shard, owner, own_slots.bit_length() - 1, core) for p in packs], 1
    )
    gather(shards, select, feats, chans)

    def store(where, strip, lanes, value):
        high, low = split(value)
        rows = pl.ds(pl.multiple_of(where * chans + strip * STRIP, STRIP), STRIP)
        uh[rows, lanes] = high
        ul[rows, lanes] = low

    for tile in range(2):
        spread(packs[tile], rot)
        rotate(rot, feats, tile * edges, store, chans)
        if tile == 0:
            saves = []
            for k, first, last in ((0, 0, 5), (1, 5, 13), (2, 13, 19)):
                for j, half in ((0, uh), (1, ul)):
                    piece = half.at[first * chans : last * chans, 0:edges]
                    at = 2 * k + j
                    saves.append(pltpu.make_async_copy(piece, u_any[at], u_sem.at[at]))
            for save in saves:
                save.start()
    for load in loads:
        load.wait()

    def product(*terms):
        left, right = [], []
        for a, b in ((zh, uh), (zh, ul), (zl, uh)):
            for sign, z, u in terms:
                first = sum(GROUPS[:z]) * chans // 2
                value = a[first : first + GROUPS[z] * chans // 2, :]
                left.append(value if sign > 0 else -value)
                right.append(b[STARTS[u] * chans : (STARTS[u] + GROUPS[u]) * chans, :])
        return nt(jnp.concatenate(left, 1), jnp.concatenate(right, 1))

    def put(at, value):
        wide = value.shape[1] // LANES
        high = value.shape[0] // own_slots // 8
        for col in range(wide):
            block = value[:, col * LANES : (col + 1) * LANES]
            full[:, at + col * high : at + (col + 1) * high] = block.reshape(own_slots, high, 8, LANES)
        return at + wide * high

    at = put(0, product((1, 0, 0)))
    at = put(at, product((1, 1, 1), (1, 2, 2)))
    at = put(at, product((1, 1, 2), (-1, 2, 1)))
    at = put(at, product((1, 3, 3), (1, 4, 4)))
    at = put(at, product((1, 3, 4), (-1, 4, 3)))
    total = full.shape[1]
    if at < total:
        full[:, at:total] = jnp.zeros((own_slots, total - at, 8, LANES), F32)
    piece = total // (2 * parts)
    rest = parts * own_slots // 4
    copies = []
    for side, target in ((0, keep_any), (1, send_any)):
        for part in range(parts):
            for slot in range(own_slots):
                first, second = part & 1, slot & 1
                lower = (part >> 1) * (own_slots // 2) + (slot >> 1)
                pos = jnp.where(core == side, first * 2 + second, second * 2 + first) * rest + lower
                begin = ((core ^ side) * parts + (tgt ^ part)) * piece
                copy = pltpu.make_async_copy(
                    full.at[slot, pl.ds(begin, piece)], target.at[pos], out_sem.at[len(copies)]
                )
                copy.start()
                copies.append(copy)
    for copy in copies + saves:
        copy.wait()


def back_zero_kernel(w, uh, ul, out):
    wh, wl = split(w[...])
    high, low = uh[...], ul[...]
    out[...] = nn(jnp.concatenate([wh, wh, wl], 1), jnp.concatenate([high, low, high], 0))


def back_pair_kernel(re, im, uh, ul, out):
    size = re.shape[0]
    rh, rl = split(re[...])
    ih, il = split(im[...])
    ph, mh = uh[0:size, :], uh[size : 2 * size, :]
    pl_, ml = ul[0:size, :], ul[size : 2 * size, :]
    w = jnp.concatenate([rh, ih, rh, ih, rl, il], 1)
    out[0:size, :] = nn(w, jnp.concatenate([ph, mh, pl_, ml, ph, mh], 0))
    out[size : 2 * size, :] = nn(w, jnp.concatenate([mh, -ph, ml, -pl_, mh, -ph], 0))


def scatter_kernel(count, shard, chans, me, pack, d0, d1, d2, out, rot, back):
    edges = rot.shape[2]
    select = onehot(ends(pack, 0, edges), count * shard, shard, me[1], twice=False)
    select = jnp.concatenate([select, select], 1)
    spread(pack, rot)
    tiles = edges // LANES
    pieces = (d0, d1, d2)
    firsts = (0, 5, 13)

    def load(where, strip, lanes):
        which = 0 if where < 5 else 1 if where < 13 else 2
        row = pl.multiple_of((where - firsts[which]) * chans + strip * 16, 16)
        return pieces[which][pl.ds(row, 16), lanes]

    def body(step, carry):
        tile = step % tiles
        strip = step // tiles
        lanes = pl.ds(pl.multiple_of(tile * LANES, LANES), LANES)
        for level in range(5):
            order = min(level, 2)
            cols = 2 * level + 1
            d = [load(place(level, r - order), strip, lanes) for r in range(2 * order + 1)]
            for c in range(cols):
                acc = [None, None]
                for r in range(2 * order + 1):
                    factor = rot[OFFSETS[level] + r * cols + c, :, lanes]
                    for half in range(2):
                        term = factor * d[r][half * 8 : half * 8 + 8]
                        acc[half] = term if r == 0 else acc[half] + term
                row = pl.multiple_of((level * level + c) * chans + strip * 16, 16)
                back[pl.ds(row, 16), lanes] = jnp.concatenate(acc, 0)
        return carry

    lax.fori_loop(0, (chans // 16) * tiles, body, 0)
    for level in range(5):
        first, last = level * level * chans, (level + 1) * (level + 1) * chans
        high, low = split(back[first:last, :])
        total = nt(select, jnp.concatenate([high, low], 1))
        for part in range(count):
            out[part, :, first:last] = total[part * shard : (part + 1) * shard]


def unpack_kernel(parts, chans, me, *refs):
    mine = refs[:parts]
    other = refs[parts : 2 * parts]
    outs = refs[2 * parts : 2 * parts + 5]
    tiles = refs[2 * parts + 5]
    piece = mine[0].shape[0]
    tgt, core = me[1], me[2]
    for side, group in ((0, mine), (1, other)):
        for part in range(parts):
            begin = ((core ^ side) * parts + (tgt ^ part)) * piece
            tiles[pl.ds(begin, piece)] = group[part][...]
    at = 0
    for out in outs:
        high, wide = out.shape[0] // 8, out.shape[1] // LANES
        for col in range(wide):
            block = tiles[at : at + high].reshape(high * 8, LANES)
            out[:, col * LANES : (col + 1) * LANES] = block
            at += high


def vmem(count):
    return [pl.BlockSpec(memory_space=pltpu.VMEM)] * count


def anywhere(count):
    return [pl.BlockSpec(memory_space=pl.ANY)] * count


SMEM = [pl.BlockSpec(memory_space=pltpu.SMEM)]


def call(kernel, name, ins, outs, shapes, scratch, micros, limit):
    return pl.pallas_call(
        kernel,
        name=name,
        in_specs=ins,
        out_specs=outs,
        out_shape=shapes,
        scratch_shapes=scratch,
        compiler_params=pltpu.CompilerParams(vmem_limit_bytes=limit * 1024 * 1024),
        cost_estimate=pl.CostEstimate(
            flops=int(micros * 1_150_000_000), bytes_accessed=100_000, transcendentals=0
        ),
    )


def shape(*dims, dtype=F32):
    return jax.ShapeDtypeStruct(dims, dtype)


def local(
    sizes,
    src_feats,
    tgt_cotangent,
    rotation,
    edge_src,
    edge_tgt,
    edge_count,
    w_zero,
    w_one_re,
    w_one_im,
    w_two_re,
    w_two_im,
):
    reps, nsrc, ntgt = sizes
    chans = w_zero.shape[0] // 5
    shard, feat = src_feats.shape[1], src_feats.shape[2]
    edges = edge_src.shape[-1]
    slots = nsrc // 2
    src_bits = nsrc.bit_length() - 1
    tgt_bits = ntgt.bit_length() - 1
    me_src, me_tgt, me_rep = (lax.axis_index(a).astype(jnp.int32) for a in ("src", "tgt", "rep"))
    me = jnp.stack([me_src, me_tgt, me_rep])

    def hop(value, axes, *routes):
        pairs = []
        for rep in range(reps):
            s_mask, t_mask = routes[rep % len(routes)]
            for s in range(nsrc):
                for t in range(ntgt):
                    base = rep * nsrc * ntgt
                    pairs.append((base + s * ntgt + t, base + (s ^ s_mask) * ntgt + (t ^ t_mask)))
        return lax.ppermute(value, AXES, pairs)

    def cross(value):
        half = nsrc * ntgt
        return lax.ppermute(value, AXES, [(i, (i + half) % (2 * half)) for i in range(2 * half)])

    tiles = edges // LANES
    length = -(-(ROT + 2) * tiles // 8) * 8
    pack = call(
        prepare_kernel,
        "prepare",
        SMEM + [pl.BlockSpec(memory_space=pltpu.HBM)] * 3,
        vmem(1)[0],
        shape(length, LANES),
        [
            pltpu.VMEM((1, 1, ROT, 1, edges), F32),
            pltpu.VMEM((1, 1, 1, edges), jnp.int32),
            pltpu.VMEM((1, 1, 1, edges), jnp.int32),
            pltpu.SemaphoreType.DMA((3,)),
        ],
        2,
        4,
    )(edge_count, jnp.transpose(rotation, (0, 1, 3, 2, 4)), edge_src, edge_tgt)
    x_own = src_feats[0]
    masks = [1 << b for b in range(src_bits)]
    masks[-1] |= masks[-2]
    g_parts = {0: tgt_cotangent[0]}
    for bit in range(src_bits - 1, 1, -1):
        for k, part in list(g_parts.items()):
            g_parts[k | (1 << bit)] = hop(part, None, (masks[bit], 0))
    far = [k for k in g_parts if k > 0]
    first, second = ((1, 0), (2, 0)), ((2, 0), (1, 0))
    g_parts[1] = hop(g_parts[0], None, *first)
    x_other = hop(x_own, None, (1, 0))
    x_parts = [x_own] + [hop(x_own, None, (0, t)) for t in range(1, ntgt)]
    g_parts[2] = hop(g_parts[0], None, *second)
    arrived = [g_parts[k] for k in far]
    pack_other = hop(pack, None, (1, 0))
    y_parts = [x_other] + [hop(x_other, None, (0, t)) for t in range(1, ntgt)]
    g_parts[3] = hop(g_parts[1], None, *second)
    for k, part in zip(far, arrived):
        g_parts[k] = part
        g_parts[k | 1] = hop(part, None, *first)
        g_parts[k | 2] = hop(part, None, *second)
    groups = sum(GROUPS) * chans
    z_rows = groups // 2

    def source_rows(parts, rows):
        return call(
            functools.partial(source_kernel, ntgt, shard, slots, chans),
            "source_rows",
            SMEM + vmem(ntgt + 1),
            vmem(2),
            [shape(z_rows, edges, dtype=BF16)] * 2,
            [
                pltpu.VMEM((feat, edges), F32),
                pltpu.VMEM((ROT, 8, edges), F32),
                pltpu.VMEM((z_rows, edges), F32),
            ],
            2.5,
            20,
        )(me, *parts, rows)

    z_own = list(source_rows(x_parts, pack))
    arrived = [g_parts[k | 1] for k in far]
    for k, part in zip(far, arrived):
        g_parts[k | 1] = part
        g_parts[k | 3] = hop(part, None, *second)
    z_other = source_rows(y_parts, pack_other)
    g_list = [g_parts[k] for k in range(nsrc)]

    per_slot = sum(
        (w.shape[0] // nsrc // 8) * (w.shape[1] // LANES)
        for w in (w_zero, w_one_re, w_one_im, w_two_re, w_two_im)
    )
    piece = -(-per_slot // (reps * ntgt))
    subs = ntgt * slots
    keep, send, *u = call(
        functools.partial(weight_kernel, nsrc, shard, slots, ntgt, chans),
        "weight_terms",
        SMEM + vmem(nsrc + 2) + anywhere(4),
        anywhere(8),
        [shape(subs, piece, 8, LANES)] * 2
        + [shape(k * chans, edges, dtype=BF16) for k in (5, 5, 8, 8, 6, 6)],
        [
            pltpu.VMEM((feat, 2 * edges), F32),
            pltpu.VMEM((ROT, 8, edges), F32),
            pltpu.VMEM((z_rows, 2 * edges), BF16),
            pltpu.VMEM((z_rows, 2 * edges), BF16),
            pltpu.VMEM((groups, 2 * edges), BF16),
            pltpu.VMEM((groups, 2 * edges), BF16),
            pltpu.VMEM((slots, piece * reps * ntgt, 8, LANES), F32),
            pltpu.SemaphoreType.DMA((4,)),
            pltpu.SemaphoreType.DMA((6,)),
            pltpu.SemaphoreType.DMA((2 * subs,)),
        ],
        14,
        44,
    )(me, *g_list, pack, pack_other, *z_own, *z_other)

    d0 = call(
        back_zero_kernel, "back_zero", vmem(3), vmem(1)[0], shape(5 * chans, edges), [], 3, 20
    )(w_zero, *u[0:2])
    d1 = call(
        back_pair_kernel, "back_one", vmem(4), vmem(1)[0], shape(8 * chans, edges), [], 4, 24
    )(w_one_re, w_one_im, *u[2:4])
    d2 = call(
        back_pair_kernel, "back_two", vmem(4), vmem(1)[0], shape(6 * chans, edges), [], 3, 20
    )(w_two_re, w_two_im, *u[4:6])
    routes = [((0, 1), (2, 0)), ((2, 0), (0, 1))]
    routes += [((0, 1 << b),) * 2 for b in range(tgt_bits - 1, 0, -1)]
    routes += [((masks[b], 0),) * 2 for b in range(src_bits - 1, 1, -1)]
    held, came = keep, cross(send)
    for k, route in enumerate(routes):
        half = held.shape[0] // 2
        sent = held[half:] + came[half:]
        if k == 1:
            sent, d0, d1, d2 = lax.optimization_barrier((sent, d0, d1, d2))
            atoms = call(
                functools.partial(scatter_kernel, ntgt, shard, chans),
                "source_sums",
                SMEM + vmem(4),
                vmem(1)[0],
                shape(ntgt, shard, feat),
                [pltpu.VMEM((ROT, 8, edges), F32), pltpu.VMEM((feat, edges), F32)],
                5,
                24,
            )(me, pack, d0, d1, d2)
        if k == 2:
            sent, atoms = lax.optimization_barrier((sent, atoms))
        held = held[:half] + came[:half]
        came = hop(sent, None, *route)
    final = held[0] + came[0]

    for b in range(tgt_bits - 1, -1, -1):
        half = atoms.shape[0] // 2
        atoms = atoms[:half] + hop(atoms[half:], None, (0, 1 << b))
    grad_feats = atoms

    mine = [final] + [hop(final, None, (0, t)) for t in range(1, ntgt)]
    other = [cross(m) for m in mine]
    outs = call(
        functools.partial(unpack_kernel, ntgt, chans),
        "unpack",
        SMEM + vmem(2 * ntgt),
        vmem(5),
        [
            shape(w.shape[0] // nsrc, w.shape[1])
            for w in (w_zero, w_one_re, w_one_im, w_two_re, w_two_im)
        ],
        [pltpu.VMEM((piece * reps * ntgt, 8, LANES), F32)],
        2,
        8,
    )(me, *mine, *other)
    return (grad_feats, *outs)


def solution(mesh):
    placed = (
        P("rep", ("src", "tgt"), None),
        P("rep", ("tgt", "src"), None),
        P("rep", "src", "tgt", None, None),
        P("rep", "src", "tgt", None),
        P("rep", "src", "tgt", None),
        P("rep", "src", "tgt"),
        P(),
        P(),
        P(),
        P(),
        P(),
    )
    sizes = tuple(mesh.shape[a] for a in AXES)
    return jax.shard_map(
        functools.partial(local, sizes),
        mesh=mesh,
        in_specs=placed,
        out_specs=(
            P("rep", ("src", "tgt"), None),
            P("src", None),
            P("src", None),
            P("src", None),
            P("src", None),
            P("src", None),
        ),
        check_vma=False,
    )
```
